512 devices in a mesh: sta: 32 (over x, z), seg: 8 (over y), band: 2 (over core).
Axes of the slice: x: 4, y: 8, z: 8, core: 2. Of those that a mesh axis runs over, the one named last changes fastest.
Arguments:
- raw_spectra: bfloat16 [8, 8192, 2, 8192], P('seg', 'sta', None, 'band'), may hold values from -200 to 200
- pair_list: int32 [96, 2], P('sta'), may hold values from 0 to 63, as said below
- pair_count: int32 [32], P('sta'), may hold values from 2 to 3
Outputs:
- stacked: float32 [96, 6, 128, 128], P('sta', None, ('seg', 'band'))
The draws below stay inside these ranges and needn't reach their ends.
Inputs may be any that keep to these rules, and one draw needn't show every extreme that they name: `pair_list`: row p belongs to index k = p // 3 of sta; its first block lies among blocks k * 2 to k * 2 + 1, which that index holds; its second block differs from the first by at most 2, on either side.
All inputs are finite; a program needn't handle non-finite values.
Results may differ from the reference program's by a relative error of at most 0.0048.
Values may be sent and summed in bfloat16 or wider, within the bound.
No kernel may reach another device: no remote copies, remote signals or barrier semaphores. Data moves between devices by JAX's collectives and lax.ppermute only.
A program may use at most 128 MiB of HBM per device.

```python
import math
import jax
import jax.numpy as jnp
from jax import lax

F = 8192
STA = 128
GROUP = 128
LAGS = 6
REACH = 2
BLK_DEV = 2
PAIR_CAP = 3
BLOCKS = 64
SEGS = 8


def draw_raw_spectra(key, part):
    key = jax.random.fold_in(key, 11)
    key_base, key_station, key_color = jax.random.split(key, 3)
    shape_all = (SEGS, BLOCKS * STA, 2, F)
    base = jnp.clip(jax.random.normal(key_base, shape_all, jnp.float32), -6.0, 6.0)
    station = jnp.exp(jax.random.uniform(key_station, (SEGS, BLOCKS * STA, 1, 1), jnp.float32, 0.0, math.log(10.0)))
    color = jnp.exp(jax.random.uniform(key_color, (1, 1, 1, F), jnp.float32, -1.2, 1.2))
    return (base * station * color).astype(jnp.bfloat16)


def draw_pair_list(key, part):
    key = jax.random.fold_in(key, 23)
    key_first, key_low, key_high, key_offset = jax.random.split(key, 4)
    rows = BLOCKS // BLK_DEV * PAIR_CAP
    owner = jnp.arange(rows, dtype=jnp.int32) // PAIR_CAP
    slot_number = jnp.arange(rows, dtype=jnp.int32) % PAIR_CAP
    local_random = jax.random.randint(key_first, (rows,), 0, BLK_DEV, dtype=jnp.int32)
    offset_random = jax.random.randint(key_offset, (rows,), -REACH, REACH + 1, dtype=jnp.int32)
    local_low = jax.random.randint(key_low, (rows,), 0, REACH, dtype=jnp.int32)
    offset_low = -jax.random.randint(key_low, (rows,), local_low + 1, REACH + 1, dtype=jnp.int32)
    local_high = BLK_DEV - 1 - jax.random.randint(key_high, (rows,), 0, REACH, dtype=jnp.int32)
    offset_high = jax.random.randint(key_high, (rows,), BLK_DEV - local_high, REACH + 1, dtype=jnp.int32)
    local_pick = jnp.where(slot_number == 0, local_low, jnp.where(slot_number == 1, local_high, local_random))
    offset = jnp.where(slot_number == 0, offset_low, jnp.where(slot_number == 1, offset_high, offset_random))
    first = owner * BLK_DEV + local_pick
    second = first + offset
    second = jnp.where((second < 0) | (second >= BLOCKS), first - offset, second)
    return jnp.stack([first, second], axis=1).astype(jnp.int32)


def draw_pair_count(key, part):
    key = jax.random.fold_in(key, 37)
    key_count, key_pick = jax.random.split(key, 2)
    owners = BLOCKS // BLK_DEV
    counts = jax.random.randint(key_count, (owners,), 2, PAIR_CAP, dtype=jnp.int32)
    chosen = jax.random.randint(key_pick, (), 0, owners, dtype=jnp.int32)
    return jnp.where(jnp.arange(owners, dtype=jnp.int32) == chosen, PAIR_CAP, counts).astype(jnp.int32)


def setup_inputs(seed: int = 0) -> dict:
    keys = jax.random.split(jax.random.key(seed), 4)
    raw_spectra = draw_raw_spectra(jax.random.fold_in(keys[3], 71), 0)
    pair_list = draw_pair_list(jax.random.fold_in(keys[3], 71), 0)
    pair_count = draw_pair_count(jax.random.fold_in(keys[3], 71), 0)
    return {"raw_spectra": raw_spectra, "pair_list": pair_list, "pair_count": pair_count}


epsilon = 1e-06

def whiten(values):
    shape_in = values.shape
    grouped = values.astype(jnp.float32).reshape(shape_in[:-1] + (shape_in[-1] // GROUP, GROUP))
    energy = lax.optimization_barrier(jnp.mean(grouped * grouped, axis=(-3, -1), keepdims=True))
    scaled = grouped * lax.rsqrt(energy + epsilon)
    return scaled.reshape(shape_in).astype(jnp.bfloat16)

def tables(first_bin, bin_count):
    lag_value = jnp.arange(LAGS, dtype=jnp.int32) - LAGS // 2
    bins = first_bin + jnp.arange(bin_count, dtype=jnp.int32)
    product = lag_value[:, None] * bins[None, :]
    theta = product.astype(jnp.float32) * jnp.float32(math.pi / F)
    return (jnp.cos(theta), jnp.sin(theta))

def rotate_one(left, cosine, sine_table):
    left_real = left[:, :, 0, :].astype(jnp.float32)
    left_imag = left[:, :, 1, :].astype(jnp.float32)
    rot_real = left_real * cosine - left_imag * sine_table
    rot_imag = left_real * sine_table + left_imag * cosine
    both = jnp.stack([rot_real, rot_imag], axis=2).astype(jnp.bfloat16)
    return both.reshape(both.shape[0], both.shape[1], -1)

def reference(raw_spectra, pair_list, pair_count):
    cosine, sine_table = tables(0, F)
    norm_scale = jnp.float32(1.0 / math.sqrt(F * SEGS))

    def one_slot(index):
        owner = index // PAIR_CAP
        slot_index = index % PAIR_CAP
        left_id = pair_list[index, 0]
        right_id = pair_list[index, 1]

        def compute():
            left = whiten(lax.dynamic_slice_in_dim(raw_spectra, (left_id * STA).astype(jnp.int32), STA, 1))
            right = whiten(lax.dynamic_slice_in_dim(raw_spectra, (right_id * STA).astype(jnp.int32), STA, 1))
            right_flat = right.reshape(right.shape[0], STA, -1).astype(jnp.float32)

            def one_lag(lag_index):
                rotated = rotate_one(left, cosine[lag_index], sine_table[lag_index])
                return lax.dot_general(rotated.astype(jnp.float32), right_flat, (((0, 2), (0, 2)), ((), ())), precision=lax.Precision.HIGHEST)
            sums = lax.map(one_lag, jnp.arange(LAGS, dtype=jnp.int32))
            return sums * norm_scale

        def nothing():
            return jnp.zeros((LAGS, STA, STA), jnp.float32)
        return lax.cond(slot_index < pair_count[owner], compute, nothing)
    return lax.map(one_slot, jnp.arange(pair_list.shape[0], dtype=jnp.int32))
```

```python
import functools
import math

import jax
import jax.numpy as jnp
from jax import lax
from jax.experimental import pallas as pl
from jax.experimental.pallas import tpu as pltpu
from jax.sharding import PartitionSpec as P

F = 8192
STA = 128
GROUP = 128
LAGS = 6
PAIR_CAP = 3
TURNS = 3
STEP = 512
EPSILON = 1e-06
FROM_LEFT, FROM_RIGHT, LOCAL, REMOTE, DEAD = 0, 1, 2, 3, 4
CHUNKS = (3072, 1024)


def tables(first_bin, bin_count):
    turn = 1 + jnp.arange(TURNS, dtype=jnp.int32)
    bins = first_bin + jnp.arange(bin_count, dtype=jnp.int32)
    theta = (turn[:, None] * bins[None, :]).astype(jnp.float32) * jnp.float32(math.pi / F)
    return jnp.concatenate([jnp.cos(theta), jnp.sin(theta), jnp.zeros((2, bin_count), jnp.float32)])


def whiten(values):
    real, imag = values[0].astype(jnp.float32), values[1].astype(jnp.float32)
    power = real * real + imag * imag
    parts = []
    for start in range(0, power.shape[1], GROUP):
        energy = jnp.sum(power[:, start : start + GROUP], axis=1, keepdims=True) * (1.0 / (2 * GROUP))
        scale = lax.rsqrt(energy + EPSILON)
        parts.append(
            (
                (real[:, start : start + GROUP] * scale).astype(jnp.bfloat16),
                (imag[:, start : start + GROUP] * scale).astype(jnp.bfloat16),
            )
        )
    return jnp.concatenate([p[0] for p in parts], axis=1), jnp.concatenate([p[1] for p in parts], axis=1)


def put_rotations(turned, block, real16, imag16, table, top):
    width = real16.shape[1]
    count = TURNS + 1 + top
    base = block * count * STA
    real, imag = real16.astype(jnp.float32), imag16.astype(jnp.float32)

    def put(turn, re, im):
        at = base + (turn + TURNS) * STA
        turned[at : at + STA, :width] = re
        turned[at : at + STA, width:] = im

    put(0, real16, imag16)
    for turn in range(1, TURNS + 1):
        cos, sin = table[turn - 1 : turn, :], table[TURNS + turn - 1 : TURNS + turn, :]
        real_cos, imag_sin = real * cos, imag * sin
        real_sin, imag_cos = real * sin, imag * cos
        if turn <= top:
            put(turn, (real_cos - imag_sin).astype(jnp.bfloat16), (real_sin + imag_cos).astype(jnp.bfloat16))
        put(-turn, (real_cos + imag_sin).astype(jnp.bfloat16), (imag_cos - real_sin).astype(jnp.bfloat16))


def product(rows, columns):
    return lax.dot_general(rows, columns, (((1,), (1,)), ((), ())), preferred_element_type=jnp.float32)


def local_kernel(info, first, second, table_ref, white_ref, local_ref, turned, sums):
    step = pl.program_id(0)

    @pl.when(step == 0)
    def _():
        sums[...] = jnp.zeros_like(sums)

    table = table_ref[...]
    for block, source in enumerate((first, second)):
        real16, imag16 = whiten(source)
        white_ref[block * STA : (block + 1) * STA, :STEP] = real16
        white_ref[block * STA : (block + 1) * STA, STEP:] = imag16
        put_rotations(turned, block, real16, imag16, table, TURNS - 1)
    sums[...] += product(turned[...], white_ref[...])

    @pl.when(step == pl.num_programs(0) - 1)
    def _():
        for slot in range(PAIR_CAP):
            here = info[slot] == LOCAL

            @pl.when(here)
            def _():
                row = pl.multiple_of(info[3 + slot] * (LAGS * STA), LAGS * STA)
                column = pl.multiple_of(info[6 + slot] * STA, STA)
                local_ref[slot] = sums[pl.ds(row, LAGS * STA), pl.ds(column, STA)]

            @pl.when(jnp.logical_not(here))
            def _():
                local_ref[slot] = jnp.zeros((LAGS * STA, STA), jnp.float32)


def local_part(info, first, second, table):
    bins = table.shape[1]
    steps = bins // STEP
    block = pl.BlockSpec((2, STA, STEP), lambda i, info: (0, 0, i))
    return pl.pallas_call(
        local_kernel,
        out_shape=(
            jax.ShapeDtypeStruct((2 * STA, 2 * bins), jnp.bfloat16),
            jax.ShapeDtypeStruct((PAIR_CAP, LAGS * STA, STA), jnp.float32),
        ),
        grid_spec=pltpu.PrefetchScalarGridSpec(
            num_scalar_prefetch=1,
            grid=(steps,),
            in_specs=[block, block, pl.BlockSpec((8, STEP), lambda i, info: (0, i))],
            out_specs=(
                pl.BlockSpec((2 * STA, 2 * STEP), lambda i, info: (0, i)),
                pl.BlockSpec((PAIR_CAP, LAGS * STA, STA), lambda i, info: (0, 0, 0)),
            ),
            scratch_shapes=[
                pltpu.VMEM((2 * LAGS * STA, 2 * STEP), jnp.bfloat16),
                pltpu.VMEM((2 * LAGS * STA, 2 * STA), jnp.float32),
            ],
        ),
        compiler_params=pltpu.CompilerParams(vmem_limit_bytes=32 << 20),
        cost_estimate=pl.CostEstimate(flops=2 * 2 * LAGS * STA * 2 * STA * 2 * bins, bytes_accessed=16 << 20, transcendentals=0),
        name="local_pairs",
    )(info, first, second, table)


ALL_TURNS = 2 * TURNS + 1
SUM_ROWS = 2 * ALL_TURNS * STA
OUT_ROWS = (PAIR_CAP + 2) * LAGS * 8


def accumulate(step, left, right, table_ref, white_ref, turned, sums):
    table = table_ref[...]
    for block, source in enumerate((left, right)):
        real16, imag16 = whiten(source)
        put_rotations(turned, block, real16, imag16, table, TURNS)
    sums[...] += product(turned[...], white_ref[...])


def remote_kernel(left, right, table_ref, white_ref, sums_ref, turned):
    step = pl.program_id(0)

    @pl.when(step == 0)
    def _():
        sums_ref[...] = jnp.zeros_like(sums_ref)

    accumulate(step, left, right, table_ref, white_ref, turned, sums_ref)


def last_kernel(info, left, right, table_ref, white_ref, before, local_ref, keep_ref, send_ref, turned, sums, stage):
    step = pl.program_id(0)

    @pl.when(step == 0)
    def _():
        sums[...] = before[...]

    accumulate(step, left, right, table_ref, white_ref, turned, sums)

    @pl.when(step == pl.num_programs(0) - 1)
    def _():
        def put(place, tile):
            octets = tile.reshape(8, 2, 8, STA)
            for core in range(2):
                stage[core, :, place * 8 : place * 8 + 8, :] = octets[:, core]

        for slot in range(PAIR_CAP):
            kind = info[slot]

            @pl.when(kind < LOCAL)
            def _():
                column = pl.multiple_of(info[3 + slot] * STA, STA)
                for lag in range(LAGS):
                    row = pl.multiple_of((kind * ALL_TURNS + 2 * TURNS - lag) * STA, STA)
                    put(slot * LAGS + lag, sums[pl.ds(row, STA), pl.ds(column, STA)].T)

            @pl.when(kind >= LOCAL)
            def _():
                for lag in range(LAGS):
                    put(slot * LAGS + lag, local_ref[slot, lag * STA : (lag + 1) * STA, :])

        for lag in range(LAGS):
            row = (ALL_TURNS + lag) * STA
            put(PAIR_CAP * LAGS + lag, sums[row : row + STA, :STA])
            row = lag * STA
            put((PAIR_CAP + 1) * LAGS + lag, sums[row : row + STA, STA:])
        core = info[9]
        keep_ref[...] = stage[core]
        send_ref[...] = stage[1 - core].astype(jnp.bfloat16)


def remote_specs(base, prefetch):
    block = pl.BlockSpec((2, STA, STEP), lambda i, *_: (0, 0, i))
    return [
        block,
        block,
        pl.BlockSpec((8, STEP), lambda i, *_: (0, base + i)),
        pl.BlockSpec((2 * STA, 2 * STEP), lambda i, *_: (0, base + i)),
    ]


def remote_cost(bins):
    return pl.CostEstimate(flops=2 * SUM_ROWS * 2 * STA * 2 * bins, bytes_accessed=8 << 20, transcendentals=0)


def remote_part(left, right, table, white, first_bin):
    bins = left.shape[2]
    return pl.pallas_call(
        remote_kernel,
        out_shape=jax.ShapeDtypeStruct((SUM_ROWS, 2 * STA), jnp.float32),
        grid=(bins // STEP,),
        in_specs=remote_specs(first_bin // STEP, False),
        out_specs=pl.BlockSpec((SUM_ROWS, 2 * STA), lambda i: (0, 0)),
        scratch_shapes=[pltpu.VMEM((SUM_ROWS, 2 * STEP), jnp.bfloat16)],
        compiler_params=pltpu.CompilerParams(vmem_limit_bytes=32 << 20),
        cost_estimate=remote_cost(bins),
        name="remote_pairs",
    )(left, right, table, white)


def last_part(info, left, right, table, white, before, local, first_bin):
    bins = left.shape[2]
    whole = lambda shape: pl.BlockSpec(shape, lambda i, *_: (0,) * len(shape))
    return pl.pallas_call(
        last_kernel,
        out_shape=(
            jax.ShapeDtypeStruct((8, OUT_ROWS, STA), jnp.float32),
            jax.ShapeDtypeStruct((8, OUT_ROWS, STA), jnp.bfloat16),
        ),
        grid_spec=pltpu.PrefetchScalarGridSpec(
            num_scalar_prefetch=1,
            grid=(bins // STEP,),
            in_specs=remote_specs(first_bin // STEP, True) + [whole((SUM_ROWS, 2 * STA)), whole(local.shape)],
            out_specs=(whole((8, OUT_ROWS, STA)), whole((8, OUT_ROWS, STA))),
            scratch_shapes=[
                pltpu.VMEM((SUM_ROWS, 2 * STEP), jnp.bfloat16),
                pltpu.VMEM((SUM_ROWS, 2 * STA), jnp.float32),
                pltpu.VMEM((2, 8, OUT_ROWS, STA), jnp.float32),
            ],
        ),
        compiler_params=pltpu.CompilerParams(vmem_limit_bytes=40 << 20),
        cost_estimate=remote_cost(bins),
        name="last_pairs",
    )(info, left, right, table, white, before, local)


def body(raw_spectra, pair_list, pair_count):
    bins_dev = raw_spectra.shape[3]
    sta_count = lax.axis_size("sta")
    position = lax.axis_index("sta")
    core = lax.axis_index("band")
    to_right = [(i, i + 1) for i in range(sta_count - 1)]
    to_left = [(i + 1, i) for i in range(sta_count - 1)]

    planes = []
    received = []
    start = 0
    for count in CHUNKS:
        cut = raw_spectra[0, :, :, start : start + count]
        first = jnp.transpose(cut[:STA], (1, 0, 2))
        second = jnp.transpose(cut[STA:], (1, 0, 2))
        planes.append((first, second))
        received.append((lax.ppermute(second, "sta", to_right), lax.ppermute(first, "sta", to_left)))
        start += count

    own = pair_list - position * 2
    left_id, right_id = own[:, 0], own[:, 1]
    kind = jnp.where(right_id == -1, FROM_LEFT, jnp.where(right_id == 2, FROM_RIGHT, LOCAL))
    kind = jnp.where((right_id == -2) | (right_id == 3), REMOTE, kind)
    kind = jnp.where(jnp.arange(PAIR_CAP) < pair_count[0], kind, DEAD)
    info = jnp.concatenate([kind, left_id, right_id, core[None]]).astype(jnp.int32)
    table = tables(core * bins_dev, bins_dev)

    first = jnp.concatenate([p[0] for p in planes], axis=2)
    second = jnp.concatenate([p[1] for p in planes], axis=2)
    white, local = local_part(info, first, second, table)
    before = remote_part(*received[0], table, white, 0)
    keep, send = last_part(info, *received[1], table, white, before, local, CHUNKS[0])

    other = lax.ppermute(send, "band", [(0, 1), (1, 0)])
    pieces = (keep + other.astype(jnp.float32)).astype(jnp.bfloat16)
    gathered = lax.all_to_all(pieces, "seg", 0, 0)
    scale = jnp.float32(1.0 / math.sqrt(F * raw_spectra.shape[0] * lax.axis_size("seg")))
    totals = jnp.sum(gathered.astype(jnp.float32), axis=0) * scale
    totals = totals.reshape(PAIR_CAP + 2, LAGS, 8, STA)
    from_left = lax.ppermute(totals[PAIR_CAP], "sta", to_right)
    from_right = lax.ppermute(totals[PAIR_CAP + 1], "sta", to_left)
    remote = (kind == REMOTE)[:, None, None, None]
    is_left = (right_id < 0)[:, None, None, None]
    return jnp.where(remote, jnp.where(is_left, from_left[None], from_right[None]), totals[:PAIR_CAP])


def solution(mesh):
    in_specs = (P("seg", "sta", None, "band"), P("sta", None), P("sta"))
    out_specs = P("sta", None, ("seg", "band"), None)
    return jax.shard_map(body, mesh=mesh, in_specs=in_specs, out_specs=out_specs, check_vma=False)
```

```python
import functools
import math

import jax
import jax.numpy as jnp
from jax import lax
from jax.experimental import pallas as pl
from jax.experimental.pallas import tpu as pltpu
from jax.sharding import PartitionSpec as P

F = 8192
STA = 128
GROUP = 128
LAGS = 6
PAIR_CAP = 3
TURNS = 3
STEP = 512
EPSILON = 1e-06
FROM_LEFT, FROM_RIGHT, LOCAL, REMOTE, DEAD = 0, 1, 2, 3, 4
CHUNKS = (1024, 2048, 1024)


def tables(first_bin, bin_count):
    turn = 1 + jnp.arange(TURNS, dtype=jnp.int32)
    bins = first_bin + jnp.arange(bin_count, dtype=jnp.int32)
    theta = (turn[:, None] * bins[None, :]).astype(jnp.float32) * jnp.float32(math.pi / F)
    return jnp.concatenate([jnp.cos(theta), jnp.sin(theta), jnp.zeros((2, bin_count), jnp.float32)])


def whiten(values):
    real, imag = values[0].astype(jnp.float32), values[1].astype(jnp.float32)
    power = real * real + imag * imag
    parts = []
    for start in range(0, power.shape[1], GROUP):
        energy = jnp.sum(power[:, start : start + GROUP], axis=1, keepdims=True) * (1.0 / (2 * GROUP))
        scale = lax.rsqrt(energy + EPSILON)
        parts.append(
            (
                (real[:, start : start + GROUP] * scale).astype(jnp.bfloat16),
                (imag[:, start : start + GROUP] * scale).astype(jnp.bfloat16),
            )
        )
    return jnp.concatenate([p[0] for p in parts], axis=1), jnp.concatenate([p[1] for p in parts], axis=1)


def put_parts(parts, real16, imag16, table):
    width = real16.shape[1]
    parts[:STA, :width] = real16
    parts[:STA, width:] = imag16
    real, imag = real16.astype(jnp.float32), imag16.astype(jnp.float32)
    for turn in range(TURNS):
        cos, sin = table[turn : turn + 1, :], table[TURNS + turn : TURNS + turn + 1, :]
        at = (1 + turn) * STA
        parts[at : at + STA, :width] = (real * cos).astype(jnp.bfloat16)
        parts[at : at + STA, width:] = (imag * cos).astype(jnp.bfloat16)
        at = (1 + TURNS + turn) * STA
        parts[at : at + STA, :width] = (imag * sin).astype(jnp.bfloat16)
        parts[at : at + STA, width:] = (real * -sin).astype(jnp.bfloat16)


def product(rows, columns):
    return lax.dot_general(rows, columns, (((1,), (1,)), ((), ())), preferred_element_type=jnp.float32)


PARTS = 2 * TURNS + 1
SUM_ROWS = PARTS * STA
SUMS = (2 * SUM_ROWS, 2 * STA)
TILE = LAGS * STA
OUT_ROWS = (PAIR_CAP + 2) * LAGS * 8


def lag_sum(sums, block, column, lag, first):
    turn = lag - LAGS // 2
    base = block * SUM_ROWS

    def part(index):
        row = base + index * STA
        row = row if isinstance(row, int) else pl.multiple_of(row, STA)
        return sums[pl.ds(row, STA), pl.ds(column, STA)]

    if turn == 0:
        return part(0)
    cosines, sines = part(abs(turn)), part(TURNS + abs(turn))
    return cosines - sines if (turn > 0) == first else cosines + sines


def whole(shape):
    return pl.BlockSpec(shape, lambda i, *_: (0,) * len(shape))


def params():
    return pltpu.CompilerParams(vmem_limit_bytes=60 << 20)


def cost(bins):
    return pl.CostEstimate(flops=2 * SUMS[0] * SUMS[1] * 2 * bins, bytes_accessed=8 << 20, transcendentals=0)


def slot_facts(pairs, count, slot):
    first_block = lax.axis_index("sta") * 2
    left, right = pairs[slot, 0] - first_block, pairs[slot, 1] - first_block
    kind = jnp.where(right == -1, FROM_LEFT, jnp.where(right == 2, FROM_RIGHT, LOCAL))
    kind = jnp.where((right == -2) | (right == 3), REMOTE, kind)
    return jnp.where(slot < count[0], kind, DEAD), left, right


def put_white(planes, white):
    real16, imag16 = whiten(planes)
    white[:, :STEP] = real16
    white[:, STEP:] = imag16


def split_kernel(raw, first, second, *white):
    planes = jnp.swapaxes(raw[0].astype(jnp.float32), 0, 1)
    plain = planes.astype(jnp.bfloat16)
    first[...] = plain[:, :STA]
    second[...] = plain[:, STA:]
    if white:
        put_white(planes, white[0])


def white_kernel(first, second, white):
    put_white(jnp.concatenate([first[...], second[...]], axis=1), white)


def plane_spec():
    return pl.BlockSpec((2, STA, STEP), lambda i, *_: (0, 0, i))


def white_spec():
    return pl.BlockSpec((2 * STA, 2 * STEP), lambda i, *_: (0, i))


def white_shape(count):
    return jax.ShapeDtypeStruct((2 * STA, 2 * count), jnp.bfloat16)


def split(raw_spectra, start, count, with_white):
    shape = jax.ShapeDtypeStruct((2, STA, count), jnp.bfloat16)
    return pl.pallas_call(
        split_kernel,
        out_shape=(shape, shape) + (white_shape(count),) * with_white,
        grid=(count // STEP,),
        in_specs=[pl.BlockSpec((1, 2 * STA, 2, STEP), lambda i: (0, 0, 0, start // STEP + i))],
        out_specs=(plane_spec(), plane_spec()) + (white_spec(),) * with_white,
        compiler_params=params(),
        cost_estimate=pl.CostEstimate(flops=0, bytes_accessed=24 * STA * count, transcendentals=0),
        name="split",
    )(raw_spectra)


def white_part(first, second):
    count = first.shape[2]
    return pl.pallas_call(
        white_kernel,
        out_shape=white_shape(count),
        grid=(count // STEP,),
        in_specs=[plane_spec(), plane_spec()],
        out_specs=white_spec(),
        compiler_params=params(),
        cost_estimate=pl.CostEstimate(flops=0, bytes_accessed=16 * STA * count, transcendentals=0),
        name="white",
    )(first, second)


def chunk_starts(chunks):
    starts = [0]
    for count in chunks:
        starts.append(starts[-1] + count // STEP)
    return starts


def local_kernel(starts, pairs, count, *refs):
    chunks = len(starts) - 1
    whites, (table_ref, local_ref, white, parts_first, parts_second, sums) = refs[:chunks], refs[chunks:]
    step = pl.program_id(0)
    last = pl.num_programs(0) - 1
    facts = [slot_facts(pairs, count, slot) for slot in range(PAIR_CAP)]
    here = [kind == LOCAL for kind, _, _ in facts]

    @pl.when(step == 0)
    def _():
        sums[...] = jnp.zeros_like(sums)

    for index in range(chunks):

        @pl.when((step >= starts[index]) & (step < starts[index + 1]))
        def _():
            white[...] = whites[index][...]

    table = table_ref[...]
    for block, parts in enumerate((parts_first, parts_second)):
        rows = white.at[block * STA : (block + 1) * STA, :]
        put_parts(parts, rows[:, :STEP], rows[:, STEP:], table)
    sums[:SUM_ROWS, :] += product(parts_first[...], white[...])
    sums[SUM_ROWS:, :] += product(parts_second[...], white[...])

    @pl.when(step == last)
    def _():
        for slot in range(PAIR_CAP):

            @pl.when(here[slot])
            def _():
                column = pl.multiple_of(facts[slot][2] * STA, STA)
                for lag in range(LAGS):
                    local_ref[slot, lag * STA : (lag + 1) * STA, :] = lag_sum(sums, facts[slot][1], column, lag, True)

            @pl.when(jnp.logical_not(here[slot]))
            def _():
                local_ref[slot] = jnp.zeros((TILE, STA), jnp.float32)


def local_part(pair_list, pair_count, whites, table):
    bins = table.shape[1]
    starts = chunk_starts([white.shape[1] // 2 for white in whites])

    def index(at, steps):
        return lambda i, *_: (0, jnp.clip(i - at, 0, steps - 1))

    specs = [
        pl.BlockSpec((2 * STA, 2 * STEP), index(starts[n], starts[n + 1] - starts[n])) for n in range(len(whites))
    ]
    return pl.pallas_call(
        functools.partial(local_kernel, tuple(starts)),
        out_shape=jax.ShapeDtypeStruct((PAIR_CAP, TILE, STA), jnp.float32),
        grid_spec=pltpu.PrefetchScalarGridSpec(
            num_scalar_prefetch=2,
            grid=(starts[-1],),
            in_specs=specs + [pl.BlockSpec((8, STEP), lambda i, *_: (0, i))],
            out_specs=whole((PAIR_CAP, TILE, STA)),
            scratch_shapes=[pltpu.VMEM((2 * STA, 2 * STEP), jnp.bfloat16)] + scratch(),
        ),
        compiler_params=params(),
        cost_estimate=cost(bins // 4),
        name="local_pairs",
    )(pair_list, pair_count, *whites, table)


def scratch():
    return [pltpu.VMEM((SUM_ROWS, 2 * STEP), jnp.bfloat16)] * 2 + [pltpu.VMEM(SUMS, jnp.float32)]


def accumulate(left, right, table_ref, white_ref, parts_left, parts_right, sums):
    table = table_ref[...]
    for source, parts in ((left, parts_left), (right, parts_right)):
        put_parts(parts, *whiten(source), table)
    sums[:SUM_ROWS, :] += product(parts_left[...], white_ref[...])
    sums[SUM_ROWS:, :] += product(parts_right[...], white_ref[...])


def early_kernel(left, right, table_ref, white_ref, *refs):
    before, (sums_ref, parts_left, parts_right) = refs[:-3], refs[-3:]

    @pl.when(pl.program_id(0) == 0)
    def _():
        sums_ref[...] = before[0][...] if before else jnp.zeros_like(sums_ref)

    accumulate(left, right, table_ref, white_ref, parts_left, parts_right, sums_ref)


def last_kernel(
    pairs, count, left, right, table_ref, white_ref, before, local, keep_ref, send_ref,
    parts_left, parts_right, sums, before_here, local_ref, arrived,
):
    step = pl.program_id(0)
    copies = (
        pltpu.make_async_copy(before, before_here, arrived.at[0]),
        pltpu.make_async_copy(local, local_ref, arrived.at[1]),
    )

    @pl.when(step == 0)
    def _():
        for copy in copies:
            copy.start()
        sums[...] = jnp.zeros_like(sums)

    accumulate(left, right, table_ref, white_ref, parts_left, parts_right, sums)

    @pl.when(step == pl.num_programs(0) - 1)
    def _():
        for copy in copies:
            copy.wait()
        sums[...] += before_here[...]
        even_core = lax.axis_index("band") == 0

        def put(place, tiles):
            octets = [tile.reshape(8, 2, 8, STA) for tile in tiles]
            even = jnp.concatenate([o[:, 0] for o in octets], axis=1)
            odd = jnp.concatenate([o[:, 1] for o in octets], axis=1)
            rows = slice(place * 8, place * 8 + 16)
            keep_ref[:, rows, :] = jnp.where(even_core, even, odd)
            send_ref[:, rows, :] = jnp.where(even_core, odd, even).astype(jnp.bfloat16)

        for slot in range(PAIR_CAP):
            kind, column_block, _ = slot_facts(pairs, count, slot)

            @pl.when(kind < LOCAL)
            def _():
                column = pl.multiple_of(column_block * STA, STA)
                for lag in range(0, LAGS, 2):
                    put(slot * LAGS + lag, [lag_sum(sums, kind, column, lag + n, False).T for n in range(2)])

            @pl.when(kind >= LOCAL)
            def _():
                for lag in range(0, LAGS, 2):
                    at = lag * STA
                    put(slot * LAGS + lag, [local_ref[slot, at + n * STA : at + (n + 1) * STA, :] for n in range(2)])

        for lag in range(0, LAGS, 2):
            put(PAIR_CAP * LAGS + lag, [lag_sum(sums, 1, 0, lag + n, True) for n in range(2)])
            put((PAIR_CAP + 1) * LAGS + lag, [lag_sum(sums, 0, STA, lag + n, True) for n in range(2)])


def early_part(left, right, white, table, start, *before):
    bins = left.shape[2]
    base = start // STEP
    return pl.pallas_call(
        early_kernel,
        out_shape=jax.ShapeDtypeStruct(SUMS, jnp.float32),
        grid=(bins // STEP,),
        in_specs=[
            plane_spec(),
            plane_spec(),
            pl.BlockSpec((8, STEP), lambda i: (0, base + i)),
            white_spec(),
        ]
        + [whole(SUMS)] * len(before),
        out_specs=whole(SUMS),
        scratch_shapes=scratch()[:2],
        compiler_params=params(),
        cost_estimate=cost(bins),
        name="early_pairs",
    )(left, right, table, white, *before)


def last_part(pair_list, pair_count, left, right, white, table, before, local):
    bins = left.shape[2]
    base = (table.shape[1] - bins) // STEP
    result = (8, OUT_ROWS, STA)
    there = pl.BlockSpec(memory_space=pl.ANY)
    return pl.pallas_call(
        last_kernel,
        out_shape=(jax.ShapeDtypeStruct(result, jnp.float32), jax.ShapeDtypeStruct(result, jnp.bfloat16)),
        grid_spec=pltpu.PrefetchScalarGridSpec(
            num_scalar_prefetch=2,
            grid=(bins // STEP,),
            in_specs=[
                plane_spec(),
                plane_spec(),
                pl.BlockSpec((8, STEP), lambda i, *_: (0, base + i)),
                white_spec(),
                there,
                there,
            ],
            out_specs=(whole(result), whole(result)),
            scratch_shapes=scratch()
            + [
                pltpu.VMEM(SUMS, jnp.float32),
                pltpu.VMEM(local.shape, jnp.float32),
                pltpu.SemaphoreType.DMA((2,)),
            ],
        ),
        compiler_params=params(),
        cost_estimate=cost(bins),
        name="last_pairs",
    )(pair_list, pair_count, left, right, table, white, before, local)


def body(raw_spectra, pair_list, pair_count):
    bins_dev = raw_spectra.shape[3]
    sta_count = lax.axis_size("sta")
    position = lax.axis_index("sta")
    core = lax.axis_index("band")
    to_right = [(i, i + 1) for i in range(sta_count - 1)]
    to_left = [(i + 1, i) for i in range(sta_count - 1)]

    def send(pair):
        return lax.ppermute(pair[1], "sta", to_right), lax.ppermute(pair[0], "sta", to_left)

    planes = []
    received = []
    start = 0
    rest = raw_spectra
    for index, count in enumerate(CHUNKS):
        first, second, *white = split(rest, start, count, int(index > 0))
        planes.append((first, second, white))
        if index + 1 < len(CHUNKS):
            received.append(send((first, second)))
            first, second, rest = lax.optimization_barrier((first, second, rest))
        start += count
    table = tables(core * bins_dev, bins_dev)
    head, received[0] = lax.optimization_barrier((planes[0][:2], received[0]))
    whites = [white_part(*head)] + [white[0] for _, _, white in planes[1:]]
    ending, whites[0], table = lax.optimization_barrier((planes[-1][:2], whites[0], table))
    received.append(send(ending))
    right_id = pair_list[:, 1] - position * 2
    live = jnp.arange(PAIR_CAP) < pair_count[0]
    local = lax.cond(
        jnp.any(live & (right_id >= 0) & (right_id <= 1)),
        lambda: local_part(pair_list, pair_count, whites, table),
        lambda: jnp.zeros((PAIR_CAP, TILE, STA), jnp.float32),
    )
    before = ()
    start = 0
    for count, pair, white in zip(CHUNKS[:-1], received[:-1], whites[:-1]):
        before = (early_part(*pair, white, table, start, *before),)
        start += count
    keep, send = last_part(pair_list, pair_count, *received[-1], whites[-1], table, *before, local)

    other = lax.ppermute(send, "band", [(0, 1), (1, 0)])
    pieces = (keep + other.astype(jnp.float32)).astype(jnp.bfloat16)
    gathered = lax.all_to_all(pieces, "seg", 0, 0)
    scale = jnp.float32(1.0 / math.sqrt(F * raw_spectra.shape[0] * lax.axis_size("seg")))
    totals = jnp.sum(gathered.astype(jnp.float32), axis=0) * scale
    totals = totals.reshape(PAIR_CAP + 2, LAGS, 8, STA)
    going_right = totals[PAIR_CAP]
    from_left = lax.ppermute(going_right, "sta", to_right)
    totals, going_right = lax.optimization_barrier((totals, going_right))
    from_right = lax.ppermute(totals[PAIR_CAP + 1], "sta", to_left)
    remote = (live & ((right_id == -2) | (right_id == 3)))[:, None, None, None]
    is_left = (right_id < 0)[:, None, None, None]
    return jnp.where(remote, jnp.where(is_left, from_left[None], from_right[None]), totals[:PAIR_CAP])


def solution(mesh):
    in_specs = (P("seg", "sta", None, "band"), P("sta", None), P("sta"))
    out_specs = P("sta", None, ("seg", "band"), None)
    return jax.shard_map(body, mesh=mesh, in_specs=in_specs, out_specs=out_specs, check_vma=False)
```

```python
import functools
import math

import jax
import jax.numpy as jnp
from jax import lax
from jax.experimental import pallas as pl
from jax.experimental.pallas import tpu as pltpu
from jax.sharding import PartitionSpec as P

F = 8192
STA = 128
GROUP = 128
LAGS = 6
PAIR_CAP = 3
TURNS = 3
STEP = 512
EPSILON = 1e-06
FROM_LEFT, FROM_RIGHT, LOCAL, REMOTE, DEAD = 0, 1, 2, 3, 4
CHUNKS = (1536, 1536, 1024)


def tables(first_bin, bin_count):
    turn = 1 + jnp.arange(TURNS, dtype=jnp.int32)
    bins = first_bin + jnp.arange(bin_count, dtype=jnp.int32)
    theta = (turn[:, None] * bins[None, :]).astype(jnp.float32) * jnp.float32(math.pi / F)
    return jnp.concatenate([jnp.cos(theta), jnp.sin(theta), jnp.zeros((2, bin_count), jnp.float32)])


def whiten(values):
    real, imag = values[0].astype(jnp.float32), values[1].astype(jnp.float32)
    power = real * real + imag * imag
    parts = []
    for start in range(0, power.shape[1], GROUP):
        energy = jnp.sum(power[:, start : start + GROUP], axis=1, keepdims=True) * (1.0 / (2 * GROUP))
        scale = lax.rsqrt(energy + EPSILON)
        parts.append(
            (
                (real[:, start : start + GROUP] * scale).astype(jnp.bfloat16),
                (imag[:, start : start + GROUP] * scale).astype(jnp.bfloat16),
            )
        )
    return jnp.concatenate([p[0] for p in parts], axis=1), jnp.concatenate([p[1] for p in parts], axis=1)


def put_parts(parts, real16, imag16, table):
    width = real16.shape[1]
    parts[:STA, :width] = real16
    parts[:STA, width:] = imag16
    real, imag = real16.astype(jnp.float32), imag16.astype(jnp.float32)
    for turn in range(TURNS):
        cos, sin = table[turn : turn + 1, :], table[TURNS + turn : TURNS + turn + 1, :]
        at = (1 + turn) * STA
        parts[at : at + STA, :width] = (real * cos).astype(jnp.bfloat16)
        parts[at : at + STA, width:] = (imag * cos).astype(jnp.bfloat16)
        at = (1 + TURNS + turn) * STA
        parts[at : at + STA, :width] = (imag * sin).astype(jnp.bfloat16)
        parts[at : at + STA, width:] = (real * -sin).astype(jnp.bfloat16)


def product(rows, columns):
    return lax.dot_general(rows, columns, (((1,), (1,)), ((), ())), preferred_element_type=jnp.float32)


PARTS = 2 * TURNS + 1
SUM_ROWS = PARTS * STA
SUMS = (2 * SUM_ROWS, 2 * STA)
TILE = LAGS * STA
OUT_ROWS = (PAIR_CAP + 2) * LAGS * 8


def lag_sum(sums, block, column, lag, first):
    turn = lag - LAGS // 2
    base = block * SUM_ROWS

    def part(index):
        row = base + index * STA
        row = row if isinstance(row, int) else pl.multiple_of(row, STA)
        return sums[pl.ds(row, STA), pl.ds(column, STA)]

    if turn == 0:
        return part(0)
    cosines, sines = part(abs(turn)), part(TURNS + abs(turn))
    return cosines - sines if (turn > 0) == first else cosines + sines


def whole(shape):
    return pl.BlockSpec(shape, lambda i, *_: (0,) * len(shape))


def params():
    return pltpu.CompilerParams(vmem_limit_bytes=60 << 20)


def cost(bins):
    return pl.CostEstimate(flops=2 * SUMS[0] * SUMS[1] * 2 * bins, bytes_accessed=8 << 20, transcendentals=0)


def slot_facts(pairs, count, slot):
    first_block = lax.axis_index("sta") * 2
    left, right = pairs[slot, 0] - first_block, pairs[slot, 1] - first_block
    kind = jnp.where(right == -1, FROM_LEFT, jnp.where(right == 2, FROM_RIGHT, LOCAL))
    kind = jnp.where((right == -2) | (right == 3), REMOTE, kind)
    return jnp.where(slot < count[0], kind, DEAD), left, right


def put_white(planes, white):
    real16, imag16 = whiten(planes)
    white[:, :STEP] = real16
    white[:, STEP:] = imag16


def split_kernel(raw, first, second, *white):
    planes = jnp.swapaxes(raw[0].astype(jnp.float32), 0, 1)
    plain = planes.astype(jnp.bfloat16)
    first[...] = plain[:, :STA]
    second[...] = plain[:, STA:]
    if white:
        put_white(planes, white[0])


def white_kernel(first, second, white):
    put_white(jnp.concatenate([first[...], second[...]], axis=1), white)


def plane_spec():
    return pl.BlockSpec((2, STA, STEP), lambda i, *_: (0, 0, i))


def white_spec():
    return pl.BlockSpec((2 * STA, 2 * STEP), lambda i, *_: (0, i))


def white_shape(count):
    return jax.ShapeDtypeStruct((2 * STA, 2 * count), jnp.bfloat16)


def split(raw_spectra, start, count, with_white):
    shape = jax.ShapeDtypeStruct((2, STA, count), jnp.bfloat16)
    return pl.pallas_call(
        split_kernel,
        out_shape=(shape, shape) + (white_shape(count),) * with_white,
        grid=(count // STEP,),
        in_specs=[pl.BlockSpec((1, 2 * STA, 2, STEP), lambda i: (0, 0, 0, start // STEP + i))],
        out_specs=(plane_spec(), plane_spec()) + (white_spec(),) * with_white,
        compiler_params=params(),
        cost_estimate=pl.CostEstimate(flops=0, bytes_accessed=24 * STA * count, transcendentals=0),
        name="split",
    )(raw_spectra)


def white_part(first, second):
    count = first.shape[2]
    return pl.pallas_call(
        white_kernel,
        out_shape=white_shape(count),
        grid=(count // STEP,),
        in_specs=[plane_spec(), plane_spec()],
        out_specs=white_spec(),
        compiler_params=params(),
        cost_estimate=pl.CostEstimate(flops=0, bytes_accessed=16 * STA * count, transcendentals=0),
        name="white",
    )(first, second)


def chunk_starts(chunks):
    starts = [0]
    for count in chunks:
        starts.append(starts[-1] + count // STEP)
    return starts


def local_kernel(starts, pairs, count, *refs):
    chunks = len(starts) - 1
    whites, (table_ref, local_ref, white, parts_first, parts_second, sums) = refs[:chunks], refs[chunks:]
    step = pl.program_id(0)
    last = pl.num_programs(0) - 1
    facts = [slot_facts(pairs, count, slot) for slot in range(PAIR_CAP)]
    here = [kind == LOCAL for kind, _, _ in facts]

    @pl.when(step == 0)
    def _():
        sums[...] = jnp.zeros_like(sums)

    for index in range(chunks):

        @pl.when((step >= starts[index]) & (step < starts[index + 1]))
        def _():
            white[...] = whites[index][...]

    table = table_ref[...]
    for block, parts in enumerate((parts_first, parts_second)):
        rows = white.at[block * STA : (block + 1) * STA, :]
        put_parts(parts, rows[:, :STEP], rows[:, STEP:], table)
    sums[:SUM_ROWS, :] += product(parts_first[...], white[...])
    sums[SUM_ROWS:, :] += product(parts_second[...], white[...])

    @pl.when(step == last)
    def _():
        for slot in range(PAIR_CAP):

            @pl.when(here[slot])
            def _():
                column = pl.multiple_of(facts[slot][2] * STA, STA)
                for lag in range(LAGS):
                    local_ref[slot, lag * STA : (lag + 1) * STA, :] = lag_sum(sums, facts[slot][1], column, lag, True)

            @pl.when(jnp.logical_not(here[slot]))
            def _():
                local_ref[slot] = jnp.zeros((TILE, STA), jnp.float32)


def local_part(pair_list, pair_count, whites, table):
    bins = table.shape[1]
    starts = chunk_starts([white.shape[1] // 2 for white in whites])

    def index(at, steps):
        return lambda i, *_: (0, jnp.clip(i - at, 0, steps - 1))

    specs = [
        pl.BlockSpec((2 * STA, 2 * STEP), index(starts[n], starts[n + 1] - starts[n])) for n in range(len(whites))
    ]
    return pl.pallas_call(
        functools.partial(local_kernel, tuple(starts)),
        out_shape=jax.ShapeDtypeStruct((PAIR_CAP, TILE, STA), jnp.float32),
        grid_spec=pltpu.PrefetchScalarGridSpec(
            num_scalar_prefetch=2,
            grid=(starts[-1],),
            in_specs=specs + [pl.BlockSpec((8, STEP), lambda i, *_: (0, i))],
            out_specs=whole((PAIR_CAP, TILE, STA)),
            scratch_shapes=[pltpu.VMEM((2 * STA, 2 * STEP), jnp.bfloat16)] + scratch(),
        ),
        compiler_params=params(),
        cost_estimate=cost(bins // 4),
        name="local_pairs",
    )(pair_list, pair_count, *whites, table)


def scratch():
    return [pltpu.VMEM((SUM_ROWS, 2 * STEP), jnp.bfloat16)] * 2 + [pltpu.VMEM(SUMS, jnp.float32)]


def accumulate(left, right, table_ref, white_ref, parts_left, parts_right, sums):
    table = table_ref[...]
    for source, parts in ((left, parts_left), (right, parts_right)):
        put_parts(parts, *whiten(source), table)
    sums[:SUM_ROWS, :] += product(parts_left[...], white_ref[...])
    sums[SUM_ROWS:, :] += product(parts_right[...], white_ref[...])


def early_kernel(left, right, table_ref, white_ref, *refs):
    before, (sums_ref, parts_left, parts_right) = refs[:-3], refs[-3:]

    @pl.when(pl.program_id(0) == 0)
    def _():
        sums_ref[...] = before[0][...] if before else jnp.zeros_like(sums_ref)

    accumulate(left, right, table_ref, white_ref, parts_left, parts_right, sums_ref)


def last_kernel(
    pairs, count, left, right, table_ref, white_ref, before, local, keep_ref, send_ref,
    parts_left, parts_right, sums, before_here, local_ref, arrived,
):
    step = pl.program_id(0)
    copies = (
        pltpu.make_async_copy(before, before_here, arrived.at[0]),
        pltpu.make_async_copy(local, local_ref, arrived.at[1]),
    )

    @pl.when(step == 0)
    def _():
        for copy in copies:
            copy.start()
        sums[...] = jnp.zeros_like(sums)

    accumulate(left, right, table_ref, white_ref, parts_left, parts_right, sums)

    @pl.when(step == pl.num_programs(0) - 1)
    def _():
        for copy in copies:
            copy.wait()
        sums[...] += before_here[...]
        even_core = lax.axis_index("band") == 0

        def put(place, tiles):
            octets = [tile.reshape(8, 2, 8, STA) for tile in tiles]
            even = jnp.concatenate([o[:, 0] for o in octets], axis=1)
            odd = jnp.concatenate([o[:, 1] for o in octets], axis=1)
            rows = pl.ds(place * 8 if isinstance(place, int) else pl.multiple_of(place * 8, 16), 16)
            keep_ref[:, rows, :] = jnp.where(even_core, even, odd)
            send_ref[:, rows, :] = jnp.where(even_core, odd, even).astype(jnp.bfloat16)

        for slot in range(PAIR_CAP):
            kind, column_block, _ = slot_facts(pairs, count, slot)

            @pl.when(kind < LOCAL)
            def _():
                column = pl.multiple_of(column_block * STA, STA)
                for lag in range(0, LAGS, 2):
                    put(slot * LAGS + lag, [lag_sum(sums, kind, column, lag + n, False).T for n in range(2)])

            @pl.when(kind >= LOCAL)
            def _():
                for lag in range(0, LAGS, 2):
                    at = lag * STA
                    put(slot * LAGS + lag, [local_ref[slot, at + n * STA : at + (n + 1) * STA, :] for n in range(2)])

        odd_place = lax.axis_index("sta") % 2
        for side, (block, column) in enumerate(((1, 0), (0, STA))):
            base = (PAIR_CAP + (odd_place + side) % 2) * LAGS
            for lag in range(0, LAGS, 2):
                put(base + lag, [lag_sum(sums, block, column, lag + n, True) for n in range(2)])


def early_part(left, right, white, table, start, *before):
    bins = left.shape[2]
    base = start // STEP
    return pl.pallas_call(
        early_kernel,
        out_shape=jax.ShapeDtypeStruct(SUMS, jnp.float32),
        grid=(bins // STEP,),
        in_specs=[
            plane_spec(),
            plane_spec(),
            pl.BlockSpec((8, STEP), lambda i: (0, base + i)),
            white_spec(),
        ]
        + [whole(SUMS)] * len(before),
        out_specs=whole(SUMS),
        scratch_shapes=scratch()[:2],
        compiler_params=params(),
        cost_estimate=cost(bins),
        name="early_pairs",
    )(left, right, table, white, *before)


def last_part(pair_list, pair_count, left, right, white, table, before, local):
    bins = left.shape[2]
    base = (table.shape[1] - bins) // STEP
    result = (8, OUT_ROWS, STA)
    there = pl.BlockSpec(memory_space=pl.ANY)
    return pl.pallas_call(
        last_kernel,
        out_shape=(jax.ShapeDtypeStruct(result, jnp.float32), jax.ShapeDtypeStruct(result, jnp.bfloat16)),
        grid_spec=pltpu.PrefetchScalarGridSpec(
            num_scalar_prefetch=2,
            grid=(bins // STEP,),
            in_specs=[
                plane_spec(),
                plane_spec(),
                pl.BlockSpec((8, STEP), lambda i, *_: (0, base + i)),
                white_spec(),
                there,
                there,
            ],
            out_specs=(whole(result), whole(result)),
            scratch_shapes=scratch()
            + [
                pltpu.VMEM(SUMS, jnp.float32),
                pltpu.VMEM(local.shape, jnp.float32),
                pltpu.SemaphoreType.DMA((2,)),
            ],
        ),
        compiler_params=params(),
        cost_estimate=cost(bins),
        name="last_pairs",
    )(pair_list, pair_count, left, right, table, white, before, local)


def body(raw_spectra, pair_list, pair_count):
    bins_dev = raw_spectra.shape[3]
    sta_count = lax.axis_size("sta")
    position = lax.axis_index("sta")
    core = lax.axis_index("band")
    to_right = [(i, i + 1) for i in range(sta_count - 1)]
    to_left = [(i + 1, i) for i in range(sta_count - 1)]

    def send(pair):
        return lax.ppermute(pair[1], "sta", to_right), lax.ppermute(pair[0], "sta", to_left)

    planes = []
    received = []
    start = 0
    rest = raw_spectra
    for index, count in enumerate(CHUNKS):
        first, second, *white = split(rest, start, count, int(index > 0))
        planes.append((first, second, white))
        if index + 1 < len(CHUNKS):
            received.append(send((first, second)))
            first, second, rest = lax.optimization_barrier((first, second, rest))
        start += count
    table = tables(core * bins_dev, bins_dev)
    head, received[0] = lax.optimization_barrier((planes[0][:2], received[0]))
    whites = [white_part(*head)] + [white[0] for _, _, white in planes[1:]]
    before = early_part(*received[0], whites[0], table, 0)
    ending, before = lax.optimization_barrier((planes[-1][:2], before))
    received.append(send(ending))
    right_id = pair_list[:, 1] - position * 2
    live = jnp.arange(PAIR_CAP) < pair_count[0]
    local = lax.cond(
        jnp.any(live & (right_id >= 0) & (right_id <= 1)),
        lambda: local_part(pair_list, pair_count, whites, table),
        lambda: jnp.zeros((PAIR_CAP, TILE, STA), jnp.float32),
    )
    start = CHUNKS[0]
    for count, pair, white in zip(CHUNKS[1:-1], received[1:-1], whites[1:-1]):
        before = early_part(*pair, white, table, start, before)
        start += count
    keep, send_half = last_part(pair_list, pair_count, *received[-1], whites[-1], table, before, local)

    other = lax.ppermute(send_half, "band", [(0, 1), (1, 0)])
    own_rows = PAIR_CAP * LAGS * 8

    def summed(start, count):
        rows = slice(start, start + count)
        return (keep[:, rows] + other[:, rows].astype(jnp.float32)).astype(jnp.bfloat16)

    swap_even = [(i, i ^ 1) for i in range(sta_count)]
    swap_odd = [(i, ((i + 1) ^ 1) - 1) for i in range(1, sta_count - 1)]
    foreign = summed(own_rows, 2 * LAGS * 8)
    got_even = lax.ppermute(foreign[:, : LAGS * 8], "sta", swap_even)
    got_odd = lax.ppermute(foreign[:, LAGS * 8 :], "sta", swap_odd)
    far = (live & ((right_id == -2) | (right_id == 3)))[None, :, None, None]
    over_even = ((right_id < 0) == (position % 2 == 1))[None, :, None, None]
    own = summed(0, own_rows).reshape(8, PAIR_CAP, LAGS * 8, STA)
    pieces = jnp.where(far, jnp.where(over_even, got_even[:, None], got_odd[:, None]), own)
    gathered = lax.all_to_all(pieces.reshape(8, own_rows, STA), "seg", 0, 0)
    scale = jnp.float32(1.0 / math.sqrt(F * raw_spectra.shape[0] * lax.axis_size("seg")))
    totals = jnp.sum(gathered.astype(jnp.float32), axis=0) * scale
    return totals.reshape(PAIR_CAP, LAGS, 8, STA)


def solution(mesh):
    in_specs = (P("seg", "sta", None, "band"), P("sta", None), P("sta"))
    out_specs = P("sta", None, ("seg", "band"), None)
    return jax.shard_map(body, mesh=mesh, in_specs=in_specs, out_specs=out_specs, check_vma=False)
```

```python
import functools
import math

import jax
import jax.numpy as jnp
from jax import lax
from jax.experimental import pallas as pl
from jax.experimental.pallas import tpu as pltpu
from jax.sharding import PartitionSpec as P

F = 8192
STA = 128
GROUP = 128
LAGS = 6
PAIR_CAP = 3
TURNS = 3
STEP = 512
EPSILON = 1e-06
FROM_LEFT, FROM_RIGHT, LOCAL, REMOTE, DEAD = 0, 1, 2, 3, 4
CHUNKS = (1536, 1536, 1024)


def tables(first_bin, bin_count):
    turn = 1 + jnp.arange(TURNS, dtype=jnp.int32)
    bins = first_bin + jnp.arange(bin_count, dtype=jnp.int32)
    theta = (turn[:, None] * bins[None, :]).astype(jnp.float32) * jnp.float32(math.pi / F)
    return jnp.concatenate([jnp.cos(theta), jnp.sin(theta), jnp.zeros((2, bin_count), jnp.float32)])


def whiten(values):
    real, imag = values[0].astype(jnp.float32), values[1].astype(jnp.float32)
    power = real * real + imag * imag
    parts = []
    for start in range(0, power.shape[1], GROUP):
        energy = jnp.sum(power[:, start : start + GROUP], axis=1, keepdims=True) * (1.0 / (2 * GROUP))
        scale = lax.rsqrt(energy + EPSILON)
        parts.append(
            (
                (real[:, start : start + GROUP] * scale).astype(jnp.bfloat16),
                (imag[:, start : start + GROUP] * scale).astype(jnp.bfloat16),
            )
        )
    return jnp.concatenate([p[0] for p in parts], axis=1), jnp.concatenate([p[1] for p in parts], axis=1)


def put_parts(parts, real16, imag16, table):
    width = real16.shape[1]
    parts[:STA, :width] = real16
    parts[:STA, width:] = imag16
    real, imag = real16.astype(jnp.float32), imag16.astype(jnp.float32)
    for turn in range(TURNS):
        cos, sin = table[turn : turn + 1, :], table[TURNS + turn : TURNS + turn + 1, :]
        at = (1 + turn) * STA
        parts[at : at + STA, :width] = (real * cos).astype(jnp.bfloat16)
        parts[at : at + STA, width:] = (imag * cos).astype(jnp.bfloat16)
        at = (1 + TURNS + turn) * STA
        parts[at : at + STA, :width] = (imag * sin).astype(jnp.bfloat16)
        parts[at : at + STA, width:] = (real * -sin).astype(jnp.bfloat16)


def product(rows, columns):
    return lax.dot_general(rows, columns, (((1,), (1,)), ((), ())), preferred_element_type=jnp.float32)


PARTS = 2 * TURNS + 1
SUM_ROWS = PARTS * STA
SUMS = (2 * SUM_ROWS, 2 * STA)
TILE = LAGS * STA
OUT_ROWS = (PAIR_CAP + 2) * LAGS * 8


def lag_sum(sums, block, column, lag, first):
    turn = lag - LAGS // 2
    base = block * SUM_ROWS

    def part(index):
        row = base + index * STA
        row = row if isinstance(row, int) else pl.multiple_of(row, STA)
        return sums[pl.ds(row, STA), pl.ds(column, STA)]

    if turn == 0:
        return part(0)
    cosines, sines = part(abs(turn)), part(TURNS + abs(turn))
    return cosines - sines if (turn > 0) == first else cosines + sines


def whole(shape):
    return pl.BlockSpec(shape, lambda i, *_: (0,) * len(shape))


def params():
    return pltpu.CompilerParams(vmem_limit_bytes=60 << 20)


def cost(bins):
    return pl.CostEstimate(flops=2 * SUMS[0] * SUMS[1] * 2 * bins, bytes_accessed=8 << 20, transcendentals=0)


def slot_facts(slots, slot):
    first_block = lax.axis_index("sta") * 2
    left, right = slots[2 * slot] - first_block, slots[2 * slot + 1] - first_block
    kind = jnp.where(right == -1, FROM_LEFT, jnp.where(right == 2, FROM_RIGHT, LOCAL))
    kind = jnp.where((right == -2) | (right == 3), REMOTE, kind)
    return jnp.where(slot < slots[2 * PAIR_CAP], kind, DEAD), left, right


def put_white(planes, white):
    real16, imag16 = whiten(planes)
    white[:, :STEP] = real16
    white[:, STEP:] = imag16


def split_kernel(raw, first, second, *white):
    planes = jnp.swapaxes(raw[0].astype(jnp.float32), 0, 1)
    plain = planes.astype(jnp.bfloat16)
    first[...] = plain[:, :STA]
    second[...] = plain[:, STA:]
    if white:
        put_white(planes, white[0])


def white_kernel(first, second, white):
    put_white(jnp.concatenate([first[...], second[...]], axis=1), white)


def plane_spec():
    return pl.BlockSpec((2, STA, STEP), lambda i, *_: (0, 0, i))


def white_spec():
    return pl.BlockSpec((2 * STA, 2 * STEP), lambda i, *_: (0, i))


def white_shape(count):
    return jax.ShapeDtypeStruct((2 * STA, 2 * count), jnp.bfloat16)


def split(raw_spectra, start, count, with_white):
    shape = jax.ShapeDtypeStruct((2, STA, count), jnp.bfloat16)
    return pl.pallas_call(
        split_kernel,
        out_shape=(shape, shape) + (white_shape(count),) * with_white,
        grid=(count // STEP,),
        in_specs=[pl.BlockSpec((1, 2 * STA, 2, STEP), lambda i: (0, 0, 0, start // STEP + i))],
        out_specs=(plane_spec(), plane_spec()) + (white_spec(),) * with_white,
        compiler_params=params(),
        cost_estimate=pl.CostEstimate(flops=0, bytes_accessed=24 * STA * count, transcendentals=0),
        name="split",
    )(raw_spectra)


def white_part(first, second):
    count = first.shape[2]
    return pl.pallas_call(
        white_kernel,
        out_shape=white_shape(count),
        grid=(count // STEP,),
        in_specs=[plane_spec(), plane_spec()],
        out_specs=white_spec(),
        compiler_params=params(),
        cost_estimate=pl.CostEstimate(flops=0, bytes_accessed=16 * STA * count, transcendentals=0),
        name="white",
    )(first, second)


def chunk_starts(chunks):
    starts = [0]
    for count in chunks:
        starts.append(starts[-1] + count // STEP)
    return starts


def local_kernel(starts, slots, *refs):
    chunks = len(starts) - 1
    whites, (table_ref, local_ref, white, parts_first, parts_second, sums) = refs[:chunks], refs[chunks:]
    step = pl.program_id(0)
    last = pl.num_programs(0) - 1
    facts = [slot_facts(slots, slot) for slot in range(PAIR_CAP)]
    here = [kind == LOCAL for kind, _, _ in facts]

    @pl.when(step == 0)
    def _():
        sums[...] = jnp.zeros_like(sums)

    for index in range(chunks):

        @pl.when((step >= starts[index]) & (step < starts[index + 1]))
        def _():
            white[...] = whites[index][...]

    table = table_ref[...]
    for block, parts in enumerate((parts_first, parts_second)):
        mine = [here[slot] & (facts[slot][1] == block) for slot in range(PAIR_CAP)]

        @pl.when(mine[0] | mine[1] | mine[2])
        def _():
            rows = white.at[block * STA : (block + 1) * STA, :]
            put_parts(parts, rows[:, :STEP], rows[:, STEP:], table)
            sums[block * SUM_ROWS : (block + 1) * SUM_ROWS, :] += product(parts[...], white[...])

    @pl.when(step == last)
    def _():
        for slot in range(PAIR_CAP):

            @pl.when(here[slot])
            def _():
                column = pl.multiple_of(facts[slot][2] * STA, STA)
                for lag in range(LAGS):
                    local_ref[slot, lag * STA : (lag + 1) * STA, :] = lag_sum(sums, facts[slot][1], column, lag, True)

            @pl.when(jnp.logical_not(here[slot]))
            def _():
                local_ref[slot] = jnp.zeros((TILE, STA), jnp.float32)


def local_part(slots, whites, table):
    bins = table.shape[1]
    starts = chunk_starts([white.shape[1] // 2 for white in whites])

    def index(at, steps):
        return lambda i, *_: (0, jnp.clip(i - at, 0, steps - 1))

    specs = [
        pl.BlockSpec((2 * STA, 2 * STEP), index(starts[n], starts[n + 1] - starts[n])) for n in range(len(whites))
    ]
    return pl.pallas_call(
        functools.partial(local_kernel, tuple(starts)),
        out_shape=jax.ShapeDtypeStruct((PAIR_CAP, TILE, STA), jnp.float32),
        grid_spec=pltpu.PrefetchScalarGridSpec(
            num_scalar_prefetch=1,
            grid=(starts[-1],),
            in_specs=specs + [pl.BlockSpec((8, STEP), lambda i, *_: (0, i))],
            out_specs=whole((PAIR_CAP, TILE, STA)),
            scratch_shapes=[pltpu.VMEM((2 * STA, 2 * STEP), jnp.bfloat16)] + scratch(),
        ),
        compiler_params=params(),
        cost_estimate=cost(bins // 4),
        name="local_pairs",
    )(slots, *whites, table)


def scratch():
    return [pltpu.VMEM((SUM_ROWS, 2 * STEP), jnp.bfloat16)] * 2 + [pltpu.VMEM(SUMS, jnp.float32)]


def accumulate(left, right, table_ref, white_ref, parts_left, parts_right, sums):
    table = table_ref[...]
    for source, parts in ((left, parts_left), (right, parts_right)):
        put_parts(parts, *whiten(source), table)
    sums[:SUM_ROWS, :] += product(parts_left[...], white_ref[...])
    sums[SUM_ROWS:, :] += product(parts_right[...], white_ref[...])


def early_kernel(left, right, table_ref, white_ref, *refs):
    before, (sums_ref, parts_left, parts_right) = refs[:-3], refs[-3:]

    @pl.when(pl.program_id(0) == 0)
    def _():
        sums_ref[...] = before[0][...] if before else jnp.zeros_like(sums_ref)

    accumulate(left, right, table_ref, white_ref, parts_left, parts_right, sums_ref)


def last_kernel(
    slots, left, right, table_ref, white_ref, before, local, keep_ref, send_ref,
    parts_left, parts_right, sums, before_here, local_ref, arrived,
):
    step = pl.program_id(0)
    copies = (
        pltpu.make_async_copy(before, before_here, arrived.at[0]),
        pltpu.make_async_copy(local, local_ref, arrived.at[1]),
    )

    @pl.when(step == 0)
    def _():
        for copy in copies:
            copy.start()
        sums[...] = jnp.zeros_like(sums)

    accumulate(left, right, table_ref, white_ref, parts_left, parts_right, sums)

    @pl.when(step == pl.num_programs(0) - 1)
    def _():
        for copy in copies:
            copy.wait()
        sums[...] += before_here[...]
        even_core = lax.axis_index("band") == 0

        def put(place, tiles):
            octets = [tile.reshape(8, 2, 8, STA) for tile in tiles]
            even = jnp.concatenate([o[:, 0] for o in octets], axis=1)
            odd = jnp.concatenate([o[:, 1] for o in octets], axis=1)
            rows = pl.ds(place * 8 if isinstance(place, int) else pl.multiple_of(place * 8, 16), 16)
            keep_ref[:, rows, :] = jnp.where(even_core, even, odd)
            send_ref[:, rows, :] = jnp.where(even_core, odd, even).astype(jnp.bfloat16)

        for slot in range(PAIR_CAP):
            kind, column_block, _ = slot_facts(slots, slot)

            @pl.when(kind < LOCAL)
            def _():
                column = pl.multiple_of(column_block * STA, STA)
                for lag in range(0, LAGS, 2):
                    put(slot * LAGS + lag, [lag_sum(sums, kind, column, lag + n, False).T for n in range(2)])

            @pl.when(kind >= LOCAL)
            def _():
                for lag in range(0, LAGS, 2):
                    at = lag * STA
                    put(slot * LAGS + lag, [local_ref[slot, at + n * STA : at + (n + 1) * STA, :] for n in range(2)])

        odd_place = lax.axis_index("sta") % 2
        for side, (block, column) in enumerate(((1, 0), (0, STA))):
            base = (PAIR_CAP + (odd_place + side) % 2) * LAGS
            for lag in range(0, LAGS, 2):
                put(base + lag, [lag_sum(sums, block, column, lag + n, True) for n in range(2)])


def early_part(left, right, white, table, start, *before):
    bins = left.shape[2]
    base = start // STEP
    return pl.pallas_call(
        early_kernel,
        out_shape=jax.ShapeDtypeStruct(SUMS, jnp.float32),
        grid=(bins // STEP,),
        in_specs=[
            plane_spec(),
            plane_spec(),
            pl.BlockSpec((8, STEP), lambda i: (0, base + i)),
            white_spec(),
        ]
        + [whole(SUMS)] * len(before),
        out_specs=whole(SUMS),
        scratch_shapes=scratch()[:2],
        compiler_params=params(),
        cost_estimate=cost(bins),
        name="early_pairs",
    )(left, right, table, white, *before)


def last_part(slots, left, right, white, table, before, local):
    bins = left.shape[2]
    base = (table.shape[1] - bins) // STEP
    result = (8, OUT_ROWS, STA)
    there = pl.BlockSpec(memory_space=pl.ANY)
    return pl.pallas_call(
        last_kernel,
        out_shape=(jax.ShapeDtypeStruct(result, jnp.float32), jax.ShapeDtypeStruct(result, jnp.bfloat16)),
        grid_spec=pltpu.PrefetchScalarGridSpec(
            num_scalar_prefetch=1,
            grid=(bins // STEP,),
            in_specs=[
                plane_spec(),
                plane_spec(),
                pl.BlockSpec((8, STEP), lambda i, *_: (0, base + i)),
                white_spec(),
                there,
                there,
            ],
            out_specs=(whole(result), whole(result)),
            scratch_shapes=scratch()
            + [
                pltpu.VMEM(SUMS, jnp.float32),
                pltpu.VMEM(local.shape, jnp.float32),
                pltpu.SemaphoreType.DMA((2,)),
            ],
        ),
        compiler_params=params(),
        cost_estimate=cost(bins),
        name="last_pairs",
    )(slots, left, right, table, white, before, local)


def body(raw_spectra, pair_list, pair_count):
    bins_dev = raw_spectra.shape[3]
    sta_count = lax.axis_size("sta")
    position = lax.axis_index("sta")
    core = lax.axis_index("band")
    to_right = [(i, i + 1) for i in range(sta_count - 1)]
    to_left = [(i + 1, i) for i in range(sta_count - 1)]

    def send(pair):
        return lax.ppermute(pair[1], "sta", to_right), lax.ppermute(pair[0], "sta", to_left)

    right_id = pair_list[:, 1] - position * 2
    live = jnp.arange(PAIR_CAP) < pair_count[0]
    any_local = jnp.any(live & (right_id >= 0) & (right_id <= 1))
    slots = jnp.concatenate([pair_list.reshape(-1), pair_count])

    planes = []
    received = []
    start = 0
    rest = raw_spectra
    for index, count in enumerate(CHUNKS):
        first, second, *white = split(rest, start, count, int(index > 0))
        planes.append((first, second, white))
        if index + 1 < len(CHUNKS):
            received.append(send((first, second)))
            first, second, rest = lax.optimization_barrier((first, second, rest))
        start += count
    table = tables(core * bins_dev, bins_dev)
    head, received[0] = lax.optimization_barrier((planes[0][:2], received[0]))
    whites = [white_part(*head)] + [white[0] for _, _, white in planes[1:]]
    before = early_part(*received[0], whites[0], table, 0)
    ending, before = lax.optimization_barrier((planes[-1][:2], before))
    received.append(send(ending))
    local = lax.cond(
        any_local,
        lambda: local_part(slots, whites, table),
        lambda: jnp.zeros((PAIR_CAP, TILE, STA), jnp.float32),
    )
    start = CHUNKS[0]
    for count, pair, white in zip(CHUNKS[1:-1], received[1:-1], whites[1:-1]):
        before = early_part(*pair, white, table, start, before)
        start += count
    keep, send_half = last_part(slots, *received[-1], whites[-1], table, before, local)

    other = lax.ppermute(send_half, "band", [(0, 1), (1, 0)])
    own_rows = PAIR_CAP * LAGS * 8

    def summed(start, count):
        rows = slice(start, start + count)
        return (keep[:, rows] + other[:, rows].astype(jnp.float32)).astype(jnp.bfloat16)

    swap_even = [(i, i ^ 1) for i in range(sta_count)]
    swap_odd = [(i, ((i + 1) ^ 1) - 1) for i in range(1, sta_count - 1)]
    foreign = summed(own_rows, 2 * LAGS * 8)
    got_even = lax.ppermute(foreign[:, : LAGS * 8], "sta", swap_even)
    got_odd = lax.ppermute(foreign[:, LAGS * 8 :], "sta", swap_odd)
    far = (live & ((right_id == -2) | (right_id == 3)))[None, :, None, None]
    over_even = ((right_id < 0) == (position % 2 == 1))[None, :, None, None]
    own = summed(0, own_rows).reshape(8, PAIR_CAP, LAGS * 8, STA)
    pieces = jnp.where(far, jnp.where(over_even, got_even[:, None], got_odd[:, None]), own)
    gathered = lax.all_to_all(pieces.reshape(8, own_rows, STA), "seg", 0, 0)
    scale = jnp.float32(1.0 / math.sqrt(F * raw_spectra.shape[0] * lax.axis_size("seg")))
    totals = jnp.sum(gathered.astype(jnp.float32), axis=0) * scale
    return totals.reshape(PAIR_CAP, LAGS, 8, STA)


def solution(mesh):
    in_specs = (P("seg", "sta", None, "band"), P("sta", None), P("sta"))
    out_specs = P("sta", None, ("seg", "band"), None)
    return jax.shard_map(body, mesh=mesh, in_specs=in_specs, out_specs=out_specs, check_vma=False)
```

```python
import functools
import math

import jax
import jax.numpy as jnp
from jax import lax
from jax.experimental import pallas as pl
from jax.experimental.pallas import tpu as pltpu
from jax.sharding import PartitionSpec as P

F = 8192
STA = 128
GROUP = 128
LAGS = 6
PAIR_CAP = 3
TURNS = 3
STEP = 512
PLAIN_STEP = 768
EPSILON = 1e-06
FROM_LEFT, FROM_RIGHT, LOCAL, REMOTE, DEAD = 0, 1, 2, 3, 4
CHUNKS = (1536, 1536, 1024)


def tables(first_bin, bin_count):
    turn = 1 + jnp.arange(TURNS, dtype=jnp.int32)
    bins = first_bin + jnp.arange(bin_count, dtype=jnp.int32)
    theta = (turn[:, None] * bins[None, :]).astype(jnp.float32) * jnp.float32(math.pi / F)
    return jnp.concatenate([jnp.cos(theta), jnp.sin(theta), jnp.zeros((2, bin_count), jnp.float32)])


def whiten(values):
    real, imag = values[0].astype(jnp.float32), values[1].astype(jnp.float32)
    power = real * real + imag * imag
    parts = []
    for start in range(0, power.shape[1], GROUP):
        energy = jnp.sum(power[:, start : start + GROUP], axis=1, keepdims=True) * (1.0 / (2 * GROUP))
        scale = lax.rsqrt(energy + EPSILON)
        parts.append(
            (
                (real[:, start : start + GROUP] * scale).astype(jnp.bfloat16),
                (imag[:, start : start + GROUP] * scale).astype(jnp.bfloat16),
            )
        )
    return jnp.concatenate([p[0] for p in parts], axis=1), jnp.concatenate([p[1] for p in parts], axis=1)


def put_parts(parts, real16, imag16, table):
    width = real16.shape[1]
    parts[:STA, :width] = real16
    parts[:STA, width:] = imag16
    real, imag = real16.astype(jnp.float32), imag16.astype(jnp.float32)
    for turn in range(TURNS):
        cos, sin = table[turn : turn + 1, :], table[TURNS + turn : TURNS + turn + 1, :]
        at = (1 + turn) * STA
        parts[at : at + STA, :width] = (real * cos).astype(jnp.bfloat16)
        parts[at : at + STA, width:] = (imag * cos).astype(jnp.bfloat16)
        at = (1 + TURNS + turn) * STA
        parts[at : at + STA, :width] = (imag * sin).astype(jnp.bfloat16)
        parts[at : at + STA, width:] = (real * -sin).astype(jnp.bfloat16)


def product(rows, columns):
    return lax.dot_general(rows, columns, (((1,), (1,)), ((), ())), preferred_element_type=jnp.float32)


PARTS = 2 * TURNS + 1
SUM_ROWS = PARTS * STA
SUMS = (2 * SUM_ROWS, 2 * STA)
TILE = LAGS * STA
OUT_ROWS = (PAIR_CAP + 2) * LAGS * 8


def lag_sum(sums, block, column, lag, first):
    turn = lag - LAGS // 2
    base = block * SUM_ROWS

    def part(index):
        row = base + index * STA
        row = row if isinstance(row, int) else pl.multiple_of(row, STA)
        return sums[pl.ds(row, STA), pl.ds(column, STA)]

    if turn == 0:
        return part(0)
    cosines, sines = part(abs(turn)), part(TURNS + abs(turn))
    return cosines - sines if (turn > 0) == first else cosines + sines


def whole(shape):
    return pl.BlockSpec(shape, lambda i, *_: (0,) * len(shape))


def params():
    return pltpu.CompilerParams(vmem_limit_bytes=60 << 20)


def cost(bins):
    return pl.CostEstimate(flops=2 * SUMS[0] * SUMS[1] * 2 * bins, bytes_accessed=8 << 20, transcendentals=0)


def slot_facts(slots, slot):
    first_block = lax.axis_index("sta") * 2
    left, right = slots[2 * slot] - first_block, slots[2 * slot + 1] - first_block
    kind = jnp.where(right == -1, FROM_LEFT, jnp.where(right == 2, FROM_RIGHT, LOCAL))
    kind = jnp.where((right == -2) | (right == 3), REMOTE, kind)
    return jnp.where(slot < slots[2 * PAIR_CAP], kind, DEAD), left, right


def put_white(planes, white):
    real16, imag16 = whiten(planes)
    white[:, :STEP] = real16
    white[:, STEP:] = imag16


def split_kernel(raw, first, second, *white):
    planes = jnp.swapaxes(raw[0].astype(jnp.float32), 0, 1)
    plain = planes.astype(jnp.bfloat16)
    first[...] = plain[:, :STA]
    second[...] = plain[:, STA:]
    if white:
        put_white(planes, white[0])


def white_kernel(first, second, white):
    put_white(jnp.concatenate([first[...], second[...]], axis=1), white)


def plane_spec():
    return pl.BlockSpec((2, STA, STEP), lambda i, *_: (0, 0, i))


def white_spec():
    return pl.BlockSpec((2 * STA, 2 * STEP), lambda i, *_: (0, i))


def white_shape(count):
    return jax.ShapeDtypeStruct((2 * STA, 2 * count), jnp.bfloat16)


def split(raw_spectra, start, count, with_white):
    shape = jax.ShapeDtypeStruct((2, STA, count), jnp.bfloat16)
    step = STEP if with_white else PLAIN_STEP
    plane = pl.BlockSpec((2, STA, step), lambda i: (0, 0, i))
    return pl.pallas_call(
        split_kernel,
        out_shape=(shape, shape) + (white_shape(count),) * with_white,
        grid=(count // step,),
        in_specs=[pl.BlockSpec((1, 2 * STA, 2, step), lambda i: (0, 0, 0, start // step + i))],
        out_specs=(plane, plane) + (white_spec(),) * with_white,
        compiler_params=params(),
        cost_estimate=pl.CostEstimate(flops=0, bytes_accessed=24 * STA * count, transcendentals=0),
        name="split",
    )(raw_spectra)


def white_part(first, second):
    count = first.shape[2]
    return pl.pallas_call(
        white_kernel,
        out_shape=white_shape(count),
        grid=(count // STEP,),
        in_specs=[plane_spec(), plane_spec()],
        out_specs=white_spec(),
        compiler_params=params(),
        cost_estimate=pl.CostEstimate(flops=0, bytes_accessed=16 * STA * count, transcendentals=0),
        name="white",
    )(first, second)


def chunk_starts(chunks):
    starts = [0]
    for count in chunks:
        starts.append(starts[-1] + count // STEP)
    return starts


def local_kernel(starts, slots, *refs):
    chunks = len(starts) - 1
    whites, (table_ref, local_ref, white, parts_first, parts_second, sums) = refs[:chunks], refs[chunks:]
    step = pl.program_id(0)
    last = pl.num_programs(0) - 1
    facts = [slot_facts(slots, slot) for slot in range(PAIR_CAP)]
    here = [kind == LOCAL for kind, _, _ in facts]

    @pl.when(step == 0)
    def _():
        sums[...] = jnp.zeros_like(sums)

    for index in range(chunks):

        @pl.when((step >= starts[index]) & (step < starts[index + 1]))
        def _():
            white[...] = whites[index][...]

    table = table_ref[...]
    for block, parts in enumerate((parts_first, parts_second)):
        mine = [here[slot] & (facts[slot][1] == block) for slot in range(PAIR_CAP)]

        @pl.when(mine[0] | mine[1] | mine[2])
        def _():
            rows = white.at[block * STA : (block + 1) * STA, :]
            put_parts(parts, rows[:, :STEP], rows[:, STEP:], table)
            sums[block * SUM_ROWS : (block + 1) * SUM_ROWS, :] += product(parts[...], white[...])

    @pl.when(step == last)
    def _():
        for slot in range(PAIR_CAP):

            @pl.when(here[slot])
            def _():
                column = pl.multiple_of(facts[slot][2] * STA, STA)
                for lag in range(LAGS):
                    local_ref[slot, lag * STA : (lag + 1) * STA, :] = lag_sum(sums, facts[slot][1], column, lag, True)

            @pl.when(jnp.logical_not(here[slot]))
            def _():
                local_ref[slot] = jnp.zeros((TILE, STA), jnp.float32)


def local_part(slots, whites, table):
    bins = table.shape[1]
    starts = chunk_starts([white.shape[1] // 2 for white in whites])

    def index(at, steps):
        return lambda i, *_: (0, jnp.clip(i - at, 0, steps - 1))

    specs = [
        pl.BlockSpec((2 * STA, 2 * STEP), index(starts[n], starts[n + 1] - starts[n])) for n in range(len(whites))
    ]
    return pl.pallas_call(
        functools.partial(local_kernel, tuple(starts)),
        out_shape=jax.ShapeDtypeStruct((PAIR_CAP, TILE, STA), jnp.float32),
        grid_spec=pltpu.PrefetchScalarGridSpec(
            num_scalar_prefetch=1,
            grid=(starts[-1],),
            in_specs=specs + [pl.BlockSpec((8, STEP), lambda i, *_: (0, i))],
            out_specs=whole((PAIR_CAP, TILE, STA)),
            scratch_shapes=[pltpu.VMEM((2 * STA, 2 * STEP), jnp.bfloat16)] + scratch(),
        ),
        compiler_params=params(),
        cost_estimate=cost(bins // 4),
        name="local_pairs",
    )(slots, *whites, table)


def scratch():
    return [pltpu.VMEM((SUM_ROWS, 2 * STEP), jnp.bfloat16)] * 2 + [pltpu.VMEM(SUMS, jnp.float32)]


def accumulate(left, right, table_ref, white_ref, parts_left, parts_right, sums):
    table = table_ref[...]
    for source, parts in ((left, parts_left), (right, parts_right)):
        put_parts(parts, *whiten(source), table)
    sums[:SUM_ROWS, :] += product(parts_left[...], white_ref[...])
    sums[SUM_ROWS:, :] += product(parts_right[...], white_ref[...])


def early_kernel(left, right, table_ref, white_ref, *refs):
    before, (sums_ref, parts_left, parts_right) = refs[:-3], refs[-3:]

    @pl.when(pl.program_id(0) == 0)
    def _():
        sums_ref[...] = before[0][...] if before else jnp.zeros_like(sums_ref)

    accumulate(left, right, table_ref, white_ref, parts_left, parts_right, sums_ref)


def last_kernel(
    slots, left, right, table_ref, white_ref, before, local, keep_ref, send_ref,
    parts_left, parts_right, sums, before_here, local_ref, arrived,
):
    step = pl.program_id(0)
    copies = (
        pltpu.make_async_copy(before, before_here, arrived.at[0]),
        pltpu.make_async_copy(local, local_ref, arrived.at[1]),
    )

    @pl.when(step == 0)
    def _():
        for copy in copies:
            copy.start()
        sums[...] = jnp.zeros_like(sums)

    accumulate(left, right, table_ref, white_ref, parts_left, parts_right, sums)

    @pl.when(step == pl.num_programs(0) - 1)
    def _():
        for copy in copies:
            copy.wait()
        sums[...] += before_here[...]
        even_core = lax.axis_index("band") == 0

        def put(place, tiles):
            octets = [tile.reshape(8, 2, 8, STA) for tile in tiles]
            even = jnp.concatenate([o[:, 0] for o in octets], axis=1)
            odd = jnp.concatenate([o[:, 1] for o in octets], axis=1)
            rows = pl.ds(place * 8 if isinstance(place, int) else pl.multiple_of(place * 8, 16), 16)
            keep_ref[:, rows, :] = jnp.where(even_core, even, odd)
            send_ref[:, rows, :] = jnp.where(even_core, odd, even).astype(jnp.bfloat16)

        for slot in range(PAIR_CAP):
            kind, column_block, _ = slot_facts(slots, slot)

            @pl.when(kind < LOCAL)
            def _():
                column = pl.multiple_of(column_block * STA, STA)
                for lag in range(0, LAGS, 2):
                    put(slot * LAGS + lag, [lag_sum(sums, kind, column, lag + n, False).T for n in range(2)])

            @pl.when(kind >= LOCAL)
            def _():
                for lag in range(0, LAGS, 2):
                    at = lag * STA
                    put(slot * LAGS + lag, [local_ref[slot, at + n * STA : at + (n + 1) * STA, :] for n in range(2)])

        odd_place = lax.axis_index("sta") % 2
        for side, (block, column) in enumerate(((1, 0), (0, STA))):
            base = (PAIR_CAP + (odd_place + side) % 2) * LAGS
            for lag in range(0, LAGS, 2):
                put(base + lag, [lag_sum(sums, block, column, lag + n, True) for n in range(2)])


def early_part(left, right, white, table, start, *before):
    bins = left.shape[2]
    base = start // STEP
    return pl.pallas_call(
        early_kernel,
        out_shape=jax.ShapeDtypeStruct(SUMS, jnp.float32),
        grid=(bins // STEP,),
        in_specs=[
            plane_spec(),
            plane_spec(),
            pl.BlockSpec((8, STEP), lambda i: (0, base + i)),
            white_spec(),
        ]
        + [whole(SUMS)] * len(before),
        out_specs=whole(SUMS),
        scratch_shapes=scratch()[:2],
        compiler_params=params(),
        cost_estimate=cost(bins),
        name="early_pairs",
    )(left, right, table, white, *before)


def last_part(slots, left, right, white, table, before, local):
    bins = left.shape[2]
    base = (table.shape[1] - bins) // STEP
    result = (8, OUT_ROWS, STA)
    there = pl.BlockSpec(memory_space=pl.ANY)
    return pl.pallas_call(
        last_kernel,
        out_shape=(jax.ShapeDtypeStruct(result, jnp.float32), jax.ShapeDtypeStruct(result, jnp.bfloat16)),
        grid_spec=pltpu.PrefetchScalarGridSpec(
            num_scalar_prefetch=1,
            grid=(bins // STEP,),
            in_specs=[
                plane_spec(),
                plane_spec(),
                pl.BlockSpec((8, STEP), lambda i, *_: (0, base + i)),
                white_spec(),
                there,
                there,
            ],
            out_specs=(whole(result), whole(result)),
            scratch_shapes=scratch()
            + [
                pltpu.VMEM(SUMS, jnp.float32),
                pltpu.VMEM(local.shape, jnp.float32),
                pltpu.SemaphoreType.DMA((2,)),
            ],
        ),
        compiler_params=params(),
        cost_estimate=cost(bins),
        name="last_pairs",
    )(slots, left, right, table, white, before, local)


def body(raw_spectra, pair_list, pair_count):
    bins_dev = raw_spectra.shape[3]
    sta_count = lax.axis_size("sta")
    position = lax.axis_index("sta")
    core = lax.axis_index("band")
    to_right = [(i, i + 1) for i in range(sta_count - 1)]
    to_left = [(i + 1, i) for i in range(sta_count - 1)]

    def send(pair):
        return lax.ppermute(pair[1], "sta", to_right), lax.ppermute(pair[0], "sta", to_left)

    right_id = pair_list[:, 1] - position * 2
    live = jnp.arange(PAIR_CAP) < pair_count[0]
    any_local = jnp.any(live & (right_id >= 0) & (right_id <= 1))
    slots = jnp.concatenate([pair_list.reshape(-1), pair_count])

    planes = []
    received = []
    start = 0
    rest = raw_spectra
    for index, count in enumerate(CHUNKS):
        first, second, *white = split(rest, start, count, int(index > 0))
        planes.append((first, second, white))
        if index + 1 < len(CHUNKS):
            received.append(send((first, second)))
            first, second, rest = lax.optimization_barrier((first, second, rest))
        start += count
    table = tables(core * bins_dev, bins_dev)
    head, received[0] = lax.optimization_barrier((planes[0][:2], received[0]))
    whites = [white_part(*head)] + [white[0] for _, _, white in planes[1:]]
    before = early_part(*received[0], whites[0], table, 0)
    ending, before = lax.optimization_barrier((planes[-1][:2], before))
    received.append(send(ending))
    local = lax.cond(
        any_local,
        lambda: local_part(slots, whites, table),
        lambda: jnp.zeros((PAIR_CAP, TILE, STA), jnp.float32),
    )
    start = CHUNKS[0]
    for count, pair, white in zip(CHUNKS[1:-1], received[1:-1], whites[1:-1]):
        before = early_part(*pair, white, table, start, before)
        start += count
    keep, send_half = last_part(slots, *received[-1], whites[-1], table, before, local)

    other = lax.ppermute(send_half, "band", [(0, 1), (1, 0)])
    own_rows = PAIR_CAP * LAGS * 8

    def summed(start, count):
        rows = slice(start, start + count)
        return (keep[:, rows] + other[:, rows].astype(jnp.float32)).astype(jnp.bfloat16)

    swap_even = [(i, i ^ 1) for i in range(sta_count)]
    swap_odd = [(i, ((i + 1) ^ 1) - 1) for i in range(1, sta_count - 1)]
    foreign = summed(own_rows, 2 * LAGS * 8)
    got_even = lax.ppermute(foreign[:, : LAGS * 8], "sta", swap_even)
    got_odd = lax.ppermute(foreign[:, LAGS * 8 :], "sta", swap_odd)
    far = (live & ((right_id == -2) | (right_id == 3)))[None, :, None, None]
    over_even = ((right_id < 0) == (position % 2 == 1))[None, :, None, None]
    own = summed(0, own_rows).reshape(8, PAIR_CAP, LAGS * 8, STA)
    pieces = jnp.where(far, jnp.where(over_even, got_even[:, None], got_odd[:, None]), own)
    gathered = lax.all_to_all(pieces.reshape(8, own_rows, STA), "seg", 0, 0)
    scale = jnp.float32(1.0 / math.sqrt(F * raw_spectra.shape[0] * lax.axis_size("seg")))
    totals = jnp.sum(gathered.astype(jnp.float32), axis=0) * scale
    return totals.reshape(PAIR_CAP, LAGS, 8, STA)


def solution(mesh):
    in_specs = (P("seg", "sta", None, "band"), P("sta", None), P("sta"))
    out_specs = P("sta", None, ("seg", "band"), None)
    return jax.shard_map(body, mesh=mesh, in_specs=in_specs, out_specs=out_specs, check_vma=False)
```

```python
import functools
import math

import jax
import jax.numpy as jnp
from jax import lax
from jax.experimental import pallas as pl
from jax.experimental.pallas import tpu as pltpu
from jax.sharding import PartitionSpec as P

F = 8192
STA = 128
GROUP = 128
LAGS = 6
PAIR_CAP = 3
TURNS = 3
STEP = 512
PLAIN_STEP = 768
EPSILON = 1e-06
FROM_LEFT, FROM_RIGHT, LOCAL, REMOTE, DEAD = 0, 1, 2, 3, 4
CHUNKS = (1536, 1536, 1024)


def tables(first_bin, bin_count):
    turn = 1 + jnp.arange(TURNS, dtype=jnp.int32)
    bins = first_bin + jnp.arange(bin_count, dtype=jnp.int32)
    theta = (turn[:, None] * bins[None, :]).astype(jnp.float32) * jnp.float32(math.pi / F)
    return jnp.concatenate([jnp.cos(theta), jnp.sin(theta), jnp.zeros((2, bin_count), jnp.float32)])


def whiten(values):
    real, imag = values[0].astype(jnp.float32), values[1].astype(jnp.float32)
    power = real * real + imag * imag
    parts = []
    for start in range(0, power.shape[1], GROUP):
        energy = jnp.sum(power[:, start : start + GROUP], axis=1, keepdims=True) * (1.0 / (2 * GROUP))
        scale = lax.rsqrt(energy + EPSILON)
        parts.append(
            (
                (real[:, start : start + GROUP] * scale).astype(jnp.bfloat16),
                (imag[:, start : start + GROUP] * scale).astype(jnp.bfloat16),
            )
        )
    return jnp.concatenate([p[0] for p in parts], axis=1), jnp.concatenate([p[1] for p in parts], axis=1)


def put_parts(parts, real16, imag16, table):
    width = real16.shape[1]
    parts[:STA, :width] = real16
    parts[:STA, width:] = imag16
    real, imag = real16.astype(jnp.float32), imag16.astype(jnp.float32)
    for turn in range(TURNS):
        cos, sin = table[turn : turn + 1, :], table[TURNS + turn : TURNS + turn + 1, :]
        at = (1 + turn) * STA
        parts[at : at + STA, :width] = (real * cos).astype(jnp.bfloat16)
        parts[at : at + STA, width:] = (imag * cos).astype(jnp.bfloat16)
        at = (1 + TURNS + turn) * STA
        parts[at : at + STA, :width] = (imag * sin).astype(jnp.bfloat16)
        parts[at : at + STA, width:] = (real * -sin).astype(jnp.bfloat16)


def product(rows, columns):
    return lax.dot_general(rows, columns, (((1,), (1,)), ((), ())), preferred_element_type=jnp.float32)


PARTS = 2 * TURNS + 1
SUM_ROWS = PARTS * STA
SUMS = (2 * SUM_ROWS, 2 * STA)
TILE = LAGS * STA
OUT_ROWS = (PAIR_CAP + 2) * LAGS * 8


def lag_sum(sums, block, column, lag, first):
    turn = lag - LAGS // 2
    base = block * SUM_ROWS

    def part(index):
        row = base + index * STA
        row = row if isinstance(row, int) else pl.multiple_of(row, STA)
        return sums[pl.ds(row, STA), pl.ds(column, STA)]

    if turn == 0:
        return part(0)
    cosines, sines = part(abs(turn)), part(TURNS + abs(turn))
    return cosines - sines if (turn > 0) == first else cosines + sines


def whole(shape):
    return pl.BlockSpec(shape, lambda i, *_: (0,) * len(shape))


def params():
    return pltpu.CompilerParams(vmem_limit_bytes=60 << 20)


def cost(bins):
    return pl.CostEstimate(flops=2 * SUMS[0] * SUMS[1] * 2 * bins, bytes_accessed=8 << 20, transcendentals=0)


def slot_facts(slots, slot):
    first_block = lax.axis_index("sta") * 2
    left, right = slots[2 * slot] - first_block, slots[2 * slot + 1] - first_block
    kind = jnp.where(right == -1, FROM_LEFT, jnp.where(right == 2, FROM_RIGHT, LOCAL))
    kind = jnp.where((right == -2) | (right == 3), REMOTE, kind)
    return jnp.where(slot < slots[2 * PAIR_CAP], kind, DEAD), left, right


def put_white(planes, white):
    real16, imag16 = whiten(planes)
    white[:, :STEP] = real16
    white[:, STEP:] = imag16


def split_kernel(raw, first, second, *white):
    planes = jnp.swapaxes(raw[0].astype(jnp.float32), 0, 1)
    plain = planes.astype(jnp.bfloat16)
    first[...] = plain[:, :STA]
    second[...] = plain[:, STA:]
    if white:
        put_white(planes, white[0])


def white_kernel(first, second, white):
    put_white(jnp.concatenate([first[...], second[...]], axis=1), white)


def plane_spec():
    return pl.BlockSpec((2, STA, STEP), lambda i, *_: (0, 0, i))


def white_spec():
    return pl.BlockSpec((2 * STA, 2 * STEP), lambda i, *_: (0, i))


def white_shape(count):
    return jax.ShapeDtypeStruct((2 * STA, 2 * count), jnp.bfloat16)


def split(raw_spectra, start, count, with_white):
    shape = jax.ShapeDtypeStruct((2, STA, count), jnp.bfloat16)
    step = STEP if with_white else PLAIN_STEP
    plane = pl.BlockSpec((2, STA, step), lambda i: (0, 0, i))
    return pl.pallas_call(
        split_kernel,
        out_shape=(shape, shape) + (white_shape(count),) * with_white,
        grid=(count // step,),
        in_specs=[pl.BlockSpec((1, 2 * STA, 2, step), lambda i: (0, 0, 0, start // step + i))],
        out_specs=(plane, plane) + (white_spec(),) * with_white,
        compiler_params=params(),
        cost_estimate=pl.CostEstimate(flops=0, bytes_accessed=24 * STA * count, transcendentals=0),
        name="split",
    )(raw_spectra)


def white_part(first, second):
    count = first.shape[2]
    return pl.pallas_call(
        white_kernel,
        out_shape=white_shape(count),
        grid=(count // STEP,),
        in_specs=[plane_spec(), plane_spec()],
        out_specs=white_spec(),
        compiler_params=params(),
        cost_estimate=pl.CostEstimate(flops=0, bytes_accessed=16 * STA * count, transcendentals=0),
        name="white",
    )(first, second)


def chunk_starts(chunks):
    starts = [0]
    for count in chunks:
        starts.append(starts[-1] + count // STEP)
    return starts


def local_kernel(starts, slots, *refs):
    chunks = len(starts) - 1
    whites, (table_ref, local_ref, white, parts_first, parts_second, sums) = refs[:chunks], refs[chunks:]
    step = pl.program_id(0)
    last = pl.num_programs(0) - 1
    facts = [slot_facts(slots, slot) for slot in range(PAIR_CAP)]
    here = [kind == LOCAL for kind, _, _ in facts]

    @pl.when(step == 0)
    def _():
        sums[...] = jnp.zeros_like(sums)

    for index in range(chunks):

        @pl.when((step >= starts[index]) & (step < starts[index + 1]))
        def _():
            white[...] = whites[index][...]

    table = table_ref[...]
    for block, parts in enumerate((parts_first, parts_second)):
        mine = [here[slot] & (facts[slot][1] == block) for slot in range(PAIR_CAP)]

        @pl.when(mine[0] | mine[1] | mine[2])
        def _():
            rows = white.at[block * STA : (block + 1) * STA, :]
            put_parts(parts, rows[:, :STEP], rows[:, STEP:], table)
            sums[block * SUM_ROWS : (block + 1) * SUM_ROWS, :] += product(parts[...], white[...])

    @pl.when(step == last)
    def _():
        for slot in range(PAIR_CAP):

            @pl.when(here[slot])
            def _():
                column = pl.multiple_of(facts[slot][2] * STA, STA)
                for lag in range(LAGS):
                    local_ref[slot, lag * STA : (lag + 1) * STA, :] = lag_sum(sums, facts[slot][1], column, lag, True)

            @pl.when(jnp.logical_not(here[slot]))
            def _():
                local_ref[slot] = jnp.zeros((TILE, STA), jnp.float32)


def local_part(slots, whites, table):
    bins = table.shape[1]
    starts = chunk_starts([white.shape[1] // 2 for white in whites])

    def index(at, steps):
        return lambda i, *_: (0, jnp.clip(i - at, 0, steps - 1))

    specs = [
        pl.BlockSpec((2 * STA, 2 * STEP), index(starts[n], starts[n + 1] - starts[n])) for n in range(len(whites))
    ]
    return pl.pallas_call(
        functools.partial(local_kernel, tuple(starts)),
        out_shape=jax.ShapeDtypeStruct((PAIR_CAP, TILE, STA), jnp.float32),
        grid_spec=pltpu.PrefetchScalarGridSpec(
            num_scalar_prefetch=1,
            grid=(starts[-1],),
            in_specs=specs + [pl.BlockSpec((8, STEP), lambda i, *_: (0, i))],
            out_specs=whole((PAIR_CAP, TILE, STA)),
            scratch_shapes=[pltpu.VMEM((2 * STA, 2 * STEP), jnp.bfloat16)] + scratch(),
        ),
        compiler_params=params(),
        cost_estimate=cost(bins // 4),
        name="local_pairs",
    )(slots, *whites, table)


def scratch():
    return [pltpu.VMEM((SUM_ROWS, 2 * STEP), jnp.bfloat16)] * 2 + [pltpu.VMEM(SUMS, jnp.float32)]


def accumulate(left, right, table_ref, white_ref, parts_left, parts_right, sums):
    table = table_ref[...]
    for source, parts in ((left, parts_left), (right, parts_right)):
        put_parts(parts, *whiten(source), table)
    sums[:SUM_ROWS, :] += product(parts_left[...], white_ref[...])
    sums[SUM_ROWS:, :] += product(parts_right[...], white_ref[...])


def early_kernel(left, right, table_ref, white_ref, *refs):
    before, (sums_ref, parts_left, parts_right) = refs[:-3], refs[-3:]

    @pl.when(pl.program_id(0) == 0)
    def _():
        sums_ref[...] = before[0][...] if before else jnp.zeros_like(sums_ref)

    accumulate(left, right, table_ref, white_ref, parts_left, parts_right, sums_ref)


def last_kernel(
    slots, left, right, table_ref, white_ref, before, local, keep_ref, send_ref,
    parts_left, parts_right, sums, before_here, local_ref, arrived,
):
    step = pl.program_id(0)
    copies = (
        pltpu.make_async_copy(before, before_here, arrived.at[0]),
        pltpu.make_async_copy(local, local_ref, arrived.at[1]),
    )

    @pl.when(step == 0)
    def _():
        for copy in copies:
            copy.start()
        sums[...] = jnp.zeros_like(sums)

    accumulate(left, right, table_ref, white_ref, parts_left, parts_right, sums)

    @pl.when(step == pl.num_programs(0) - 1)
    def _():
        for copy in copies:
            copy.wait()
        sums[...] += before_here[...]
        even_core = lax.axis_index("band") == 0

        def put(place, tiles):
            octets = [tile.reshape(8, 2, 8, STA) for tile in tiles]
            even = jnp.concatenate([o[:, 0] for o in octets], axis=1)
            odd = jnp.concatenate([o[:, 1] for o in octets], axis=1)
            rows = pl.ds(place * 8 if isinstance(place, int) else pl.multiple_of(place * 8, 16), 16)
            keep_ref[:, rows, :] = jnp.where(even_core, even, odd).astype(jnp.bfloat16)
            send_ref[:, rows, :] = jnp.where(even_core, odd, even).astype(jnp.bfloat16)

        for slot in range(PAIR_CAP):
            kind, column_block, _ = slot_facts(slots, slot)

            @pl.when(kind < LOCAL)
            def _():
                column = pl.multiple_of(column_block * STA, STA)
                for lag in range(0, LAGS, 2):
                    put(slot * LAGS + lag, [lag_sum(sums, kind, column, lag + n, False).T for n in range(2)])

            @pl.when(kind >= LOCAL)
            def _():
                for lag in range(0, LAGS, 2):
                    at = lag * STA
                    put(slot * LAGS + lag, [local_ref[slot, at + n * STA : at + (n + 1) * STA, :] for n in range(2)])

        odd_place = lax.axis_index("sta") % 2
        for side, (block, column) in enumerate(((1, 0), (0, STA))):
            base = (PAIR_CAP + (odd_place + side) % 2) * LAGS
            for lag in range(0, LAGS, 2):
                put(base + lag, [lag_sum(sums, block, column, lag + n, True) for n in range(2)])


def early_part(left, right, white, table, start, *before):
    bins = left.shape[2]
    base = start // STEP
    return pl.pallas_call(
        early_kernel,
        out_shape=jax.ShapeDtypeStruct(SUMS, jnp.float32),
        grid=(bins // STEP,),
        in_specs=[
            plane_spec(),
            plane_spec(),
            pl.BlockSpec((8, STEP), lambda i: (0, base + i)),
            white_spec(),
        ]
        + [whole(SUMS)] * len(before),
        out_specs=whole(SUMS),
        scratch_shapes=scratch()[:2],
        compiler_params=params(),
        cost_estimate=cost(bins),
        name="early_pairs",
    )(left, right, table, white, *before)


def last_part(slots, left, right, white, table, before, local):
    bins = left.shape[2]
    base = (table.shape[1] - bins) // STEP
    result = (8, OUT_ROWS, STA)
    there = pl.BlockSpec(memory_space=pl.ANY)
    return pl.pallas_call(
        last_kernel,
        out_shape=(jax.ShapeDtypeStruct(result, jnp.bfloat16),) * 2,
        grid_spec=pltpu.PrefetchScalarGridSpec(
            num_scalar_prefetch=1,
            grid=(bins // STEP,),
            in_specs=[
                plane_spec(),
                plane_spec(),
                pl.BlockSpec((8, STEP), lambda i, *_: (0, base + i)),
                white_spec(),
                there,
                there,
            ],
            out_specs=(whole(result), whole(result)),
            scratch_shapes=scratch()
            + [
                pltpu.VMEM(SUMS, jnp.float32),
                pltpu.VMEM(local.shape, jnp.float32),
                pltpu.SemaphoreType.DMA((2,)),
            ],
        ),
        compiler_params=params(),
        cost_estimate=cost(bins),
        name="last_pairs",
    )(slots, left, right, table, white, before, local)


def body(raw_spectra, pair_list, pair_count):
    bins_dev = raw_spectra.shape[3]
    sta_count = lax.axis_size("sta")
    position = lax.axis_index("sta")
    core = lax.axis_index("band")
    to_right = [(i, i + 1) for i in range(sta_count - 1)]
    to_left = [(i + 1, i) for i in range(sta_count - 1)]

    def send(pair):
        return lax.ppermute(pair[1], "sta", to_right), lax.ppermute(pair[0], "sta", to_left)

    right_id = pair_list[:, 1] - position * 2
    live = jnp.arange(PAIR_CAP) < pair_count[0]
    any_local = jnp.any(live & (right_id >= 0) & (right_id <= 1))
    slots = jnp.concatenate([pair_list.reshape(-1), pair_count])

    planes = []
    received = []
    start = 0
    rest = raw_spectra
    for index, count in enumerate(CHUNKS):
        first, second, *white = split(rest, start, count, int(index > 0))
        planes.append((first, second, white))
        if index + 1 < len(CHUNKS):
            received.append(send((first, second)))
            first, second, rest = lax.optimization_barrier((first, second, rest))
        start += count
    table = tables(core * bins_dev, bins_dev)
    head, received[0] = lax.optimization_barrier((planes[0][:2], received[0]))
    whites = [white_part(*head)] + [white[0] for _, _, white in planes[1:]]
    before = early_part(*received[0], whites[0], table, 0)
    ending, before = lax.optimization_barrier((planes[-1][:2], before))
    received.append(send(ending))
    local = lax.cond(
        any_local,
        lambda: local_part(slots, whites, table),
        lambda: jnp.zeros((PAIR_CAP, TILE, STA), jnp.float32),
    )
    start = CHUNKS[0]
    for count, pair, white in zip(CHUNKS[1:-1], received[1:-1], whites[1:-1]):
        before = early_part(*pair, white, table, start, before)
        start += count
    keep, send_half = last_part(slots, *received[-1], whites[-1], table, before, local)

    other = lax.ppermute(send_half, "band", [(0, 1), (1, 0)])
    own_rows = PAIR_CAP * LAGS * 8

    def summed(start, count):
        rows = slice(start, start + count)
        return (keep[:, rows].astype(jnp.float32) + other[:, rows].astype(jnp.float32)).astype(jnp.bfloat16)

    swap_even = [(i, i ^ 1) for i in range(sta_count)]
    swap_odd = [(i, ((i + 1) ^ 1) - 1) for i in range(1, sta_count - 1)]
    foreign = summed(own_rows, 2 * LAGS * 8)
    got_even = lax.ppermute(foreign[:, : LAGS * 8], "sta", swap_even)
    got_odd = lax.ppermute(foreign[:, LAGS * 8 :], "sta", swap_odd)
    far = (live & ((right_id == -2) | (right_id == 3)))[None, :, None, None]
    over_even = ((right_id < 0) == (position % 2 == 1))[None, :, None, None]
    own = summed(0, own_rows).reshape(8, PAIR_CAP, LAGS * 8, STA)
    pieces = jnp.where(far, jnp.where(over_even, got_even[:, None], got_odd[:, None]), own)
    gathered = lax.all_to_all(pieces.reshape(8, own_rows, STA), "seg", 0, 0)
    scale = jnp.float32(1.0 / math.sqrt(F * raw_spectra.shape[0] * lax.axis_size("seg")))
    totals = jnp.sum(gathered.astype(jnp.float32), axis=0) * scale
    return totals.reshape(PAIR_CAP, LAGS, 8, STA)


def solution(mesh):
    in_specs = (P("seg", "sta", None, "band"), P("sta", None), P("sta"))
    out_specs = P("sta", None, ("seg", "band"), None)
    return jax.shard_map(body, mesh=mesh, in_specs=in_specs, out_specs=out_specs, check_vma=False)
```
